256 devices in a mesh: space: 128 (over y, x, z), chan: 2 (over core).
Axes of the slice: x: 4, y: 4, z: 8, core: 2. Of those that a mesh axis runs over, the one named last changes fastest.
Arguments:
- features: bfloat16 [32, 4096, 512], P('chan', 'space'), may hold values from -6 to 6
- neighbours: int32 [4096, 6], P('space'), may hold values from -1 to 4095, as said below
- octants: int32 [4096], P('space'), may hold values from 0 to 7, as said below
- owners: int32 [512, 1], P('space'), may hold values from 0 to 15; in each aligned block of 4 rows (0 to 3, 4 to 7, ...) at most 2 rows name the same one
- coarse_field: bfloat16 [32, 4096, 512], P('chan', 'space'), may hold values from -6 to 6
- enc_weight: bfloat16 [7, 32, 32], replicated, may hold values from -0.375 to 0.375
- enc_bias: float32 [32], replicated, may hold values from -3 to 3
- coarse_weight: bfloat16 [7, 32, 32], replicated, may hold values from -0.375 to 0.375
- coarse_bias: float32 [32], replicated, may hold values from -3 to 3
- dec_weight: bfloat16 [7, 32, 32], replicated, may hold values from -0.375 to 0.375
- dec_bias: float32 [32], replicated, may hold values from -3 to 3
- psi_weight: bfloat16 [32, 3], replicated, may hold values from -1 to 1
Outputs:
- velocity: float32 [3, 4096, 512], P(None, 'space')
The draws below stay inside these ranges and needn't reach their ends.
Inputs may be any that keep to these rules, and one draw needn't show every extreme that they name: `neighbours`: an entry that is not -1 names a block of the same device, or, for one of the first 8 blocks of a device and an even direction, one of the last 8 blocks of the device before, or, for one of the last 8 blocks and an odd direction, one of the first 8 blocks of the device after. `octants`: within each run of blocks 8 K to 8 K + 7 every octant appears once. `owners`: among the 4 coarse blocks of one device at most 2 have the same owner.
All inputs are finite; a program needn't handle non-finite values.
Results may differ from the reference program's by a relative error of at most 0.01.
Values may be sent and summed in bfloat16 or wider, within the bound.
A program may use at most 128 MiB of HBM per device.

```python
import math
import jax
import jax.numpy as jnp
import numpy as np
from jax import lax

C = 32
WINDOW = 16
B_DEV = 32
BLOCKS = 4096
CB = 4
COARSE = 512
REACH = 8
PAIR = 2
OSLOTS = 32
CSLOTS = 4096
N_SPACE = 128


def draw_neighbours(key, part):
    per_dev = B_DEV
    block_count = BLOCKS
    spaces = BLOCKS // B_DEV
    reach_rows = REACH
    block_ids = jnp.arange(block_count, dtype=jnp.int32)[:, None]
    device = block_ids // per_dev
    position = block_ids % per_dev
    direction = jnp.arange(6, dtype=jnp.int32)[None, :]
    kind_key, own_key, cross_key = jax.random.split(key, 3)
    kind_pick = jax.random.randint(kind_key, (block_count, 6), 0, 4)
    own_pick = jax.random.randint(own_key, (block_count, 6), 0, per_dev)
    cross_pick = jax.random.randint(cross_key, (block_count, 6), 0, reach_rows)
    minus_ok = (position < reach_rows) & (direction % 2 == 0) & (device > 0)
    plus_ok = (position >= per_dev - reach_rows) & (direction % 2 == 1) & (device < spaces - 1)
    own_target = device * per_dev + own_pick
    lower_target = (device - 1) * per_dev + per_dev - reach_rows + cross_pick
    upper_target = (device + 1) * per_dev + cross_pick
    target = jnp.where((kind_pick == 3) & minus_ok, lower_target, jnp.where((kind_pick == 3) & plus_ok, upper_target, own_target))
    target = jnp.where(kind_pick == 0, -1, target)
    force_lower = (position == 0) & (direction == 0)
    target = jnp.where(force_lower, jnp.where(device > 0, (device - 1) * per_dev + per_dev - reach_rows, -1), target)
    force_upper = (position == per_dev - 1) & (direction == 1)
    target = jnp.where(force_upper, jnp.where(device < spaces - 1, (device + 1) * per_dev + reach_rows - 1, -1), target)
    return target.astype(jnp.int32)


def draw_octants(key, part):
    group_count = BLOCKS // 8
    scores = jax.random.randint(key, (group_count, 8), 0, 1 << 20) * 8 + jnp.arange(8, dtype=jnp.int32)[None, :]
    return jnp.argsort(scores, axis=1).astype(jnp.int32).reshape(BLOCKS)


def level_of(key, dims, cuts, least, top_value):
    gain = 1.0
    for dim, shards_of in cuts:
        steps = jax.random.uniform(jax.random.fold_in(jax.random.fold_in(key, 6), dim), (shards_of,), jnp.float32, least / len(cuts), top_value / len(cuts))
        gain = gain * jnp.repeat(jnp.exp(steps), dims[dim] // shards_of).reshape((-1,) + (1,) * (len(dims) - 1 - dim))
    return gain


def deal_out(key, own, number, rows, count, top, limit, skew):
    order = jax.random.permutation(key, count)
    heavy_load, ordinary = load_shares(count, rows * top, limit, skew, True), load_shares(count, rows * top, limit, skew, False)
    places = jnp.arange(count)

    def named(lengths, offset_by):
        used = int((lengths > 0).sum())
        fixed = max(1, used // 4)
        passed = fixed + (places - fixed + offset_by * (used - fixed)) % max(1, count - fixed)
        return jnp.zeros((count,), jnp.int32).at[order[jnp.where(places < fixed, places, passed)]].set(jnp.asarray(lengths, jnp.int32))

    lengths = jnp.where(number % 4 == 0, named(heavy_load, number // 4), named(ordinary, number - number // 4 - 1))
    mixed = jax.random.permutation(jax.random.fold_in(own, 3), count)
    donor, receiver = mixed[0:count // 2 * 2:2], mixed[1:count // 2 * 2:2]
    margin = jnp.minimum(lengths[donor] - 1, limit - lengths[receiver]) // 2
    margin = jnp.where((donor == order[0]) | (receiver == order[0]) | (lengths[receiver] == 0), 0, jnp.maximum(margin, 0))
    passed = jax.random.randint(jax.random.fold_in(own, 4), (count // 2,), 0, 1 << 20) % (margin + 1)
    lengths = lengths.at[donor].add(-passed).at[receiver].add(passed)
    items = jnp.searchsorted(jnp.cumsum(lengths), jnp.arange(rows * top), side="right").astype(jnp.int32)
    table = items.reshape(top, rows).T
    table = table[jax.random.permutation(jax.random.fold_in(own, 1), rows)]
    offset_by = jax.random.randint(jax.random.fold_in(own, 2), (rows, 1), 0, top)
    return jnp.take_along_axis(table, (jnp.arange(top)[None, :] + offset_by) % top, axis=1)


def load_shares(amount, total, reach, lean, full):
    weights = [(1 << 20) // math.isqrt(rank ** lean) + 1 for rank in range(1, amount + 1)]
    largest = reach if full else min(reach, max(-(-total // amount), total * weights[0] // sum(weights)))
    least = 1 if total - largest >= amount - 1 else 0
    holding, spare = [largest] + [least] * (amount - 1), total - largest - least * (amount - 1)
    while spare > 0:
        candidates = [i for i in range(1, amount) if holding[i] < largest] or [i for i in range(1, amount) if holding[i] < reach]
        pool, left = sum([weights[i] for i in candidates]), spare
        for i in candidates:
            extra = min(reach - holding[i], max(1, left * weights[i] // pool), spare)
            holding[i] = holding[i] + extra
            spare = spare - extra
    return np.array(holding)


def centred(rng, extent, deviation, limit, shards=(), held_as=jnp.bfloat16):
    entries = jax.random.normal(rng, extent, jnp.float32) * deviation
    if len(shards) > 0:
        entries = level_of(rng, extent, shards, -0.22, 0.18) * entries
    return jnp.clip(entries, min=-limit, max=limit).astype(held_as)


def setup_inputs(seed: int = 0) -> dict:
    streams_of = jax.random.split(jax.random.key(seed), 13)
    features = centred(streams_of[0], (C, BLOCKS, 512), 1.0, 6.0, ((0, 2), (1, 128)))
    neighbours = draw_neighbours(jax.random.fold_in(streams_of[12], 71), 0)
    octants = draw_octants(jax.random.fold_in(streams_of[12], 71), 0)
    owners_keys = jax.random.split(jax.random.fold_in(streams_of[3], 1), COARSE // CB)
    owners_turns = jax.random.permutation(jax.random.fold_in(streams_of[3], 3), COARSE // CB)
    owners = jax.vmap(lambda own, number: deal_out(jax.random.fold_in(streams_of[3], 2), own, number, CB, WINDOW, 1, PAIR, 2))(owners_keys, owners_turns).reshape((COARSE, 1))
    coarse_field = centred(streams_of[4], (C, CSLOTS, 512), 1.0, 6.0, ((0, 2), (1, 128)))
    enc_weight = centred(streams_of[5], (7, C, C), (7 * C) ** -0.5, 0.375)
    enc_bias = centred(streams_of[6], (C,), 0.5, 3.0, (), jnp.float32)
    coarse_weight = centred(streams_of[7], (7, C, C), (7 * C) ** -0.5, 0.375)
    coarse_bias = centred(streams_of[8], (C,), 0.5, 3.0, (), jnp.float32)
    dec_weight = centred(streams_of[9], (7, C, C), (7 * C) ** -0.5, 0.375)
    dec_bias = centred(streams_of[10], (C,), 0.5, 3.0, (), jnp.float32)
    psi_weight = centred(streams_of[11], (C, 3), C ** -0.5, 1.0)
    return {"features": features, "neighbours": neighbours, "octants": octants, "owners": owners, "coarse_field": coarse_field, "enc_weight": enc_weight, "enc_bias": enc_bias, "coarse_weight": coarse_weight, "coarse_bias": coarse_bias, "dec_weight": dec_weight, "dec_bias": dec_bias, "psi_weight": psi_weight}


def voxel_tables():
    voxels = np.arange(512)
    coords = [voxels // 64, (voxels // 8) % 8, voxels % 8]
    strides = [64, 8, 1]
    facepos = [(coords[1] * 8 + coords[2]).astype(np.int32), (coords[0] * 8 + coords[2]).astype(np.int32), (coords[0] * 8 + coords[1]).astype(np.int32)]
    pieces = []
    for which_axis in range(3):
        for side_value in (0, 7):
            chosen = voxels[coords[which_axis] == side_value]
            pieces.append(chosen[np.argsort(facepos[which_axis][chosen])])
    face_index = np.concatenate(pieces).astype(np.int32)
    octant_voxel = (coords[0] // 2) * 16 + (coords[1] // 2) * 4 + coords[2] // 2
    pool_matrix = (octant_voxel[:, None] == np.arange(64)[None, :]).astype(np.float32) * 0.125
    octant_id = (coords[0] // 4) * 4 + (coords[1] // 4) * 2 + coords[2] // 4
    inner_voxel = (coords[0] % 4) * 16 + (coords[1] % 4) * 4 + coords[2] % 4
    to_coarse = (octant_id * 64 + inner_voxel).astype(np.int32)
    to_octants = np.argsort(to_coarse).astype(np.int32)
    return coords, strides, facepos, face_index, pool_matrix, to_coarse, to_octants


def make_taps(block_x, near_faces, tables):
    coords, strides, facepos = tables[0], tables[1], tables[2]
    stencil = [block_x]
    for direction in range(6):
        which_axis = direction // 2
        step_sign = 1 if direction % 2 else -1
        rolled = jnp.roll(block_x, -step_sign * strides[which_axis], axis=2)
        on_edge = coords[which_axis] == (7 if step_sign > 0 else 0)
        face_fill = jnp.take(near_faces[direction], facepos[which_axis], axis=2)
        stencil.append(jnp.where(on_edge, face_fill, rolled))
    return jnp.stack(stencil)


def neighbour_faces(face_pool, index_rows):
    near_faces = []
    for direction in range(6):
        column = index_rows[:, direction]
        present = column >= 0
        opposite = direction ^ 1
        picked = jnp.take(face_pool[:, :, opposite * 64:(opposite + 1) * 64], jnp.where(present, column, 0), axis=1)
        near_faces.append(jnp.where(present[None, :, None], picked, jnp.zeros((), picked.dtype)))
    return near_faces


def derivative(stencil, axis_id, component):
    return (stencil[2 + 2 * axis_id, component].astype(jnp.float32) - stencil[1 + 2 * axis_id, component].astype(jnp.float32)) * 0.5


def curl_field(stencil):
    return jnp.stack([derivative(stencil, 1, 2) - derivative(stencil, 2, 1), derivative(stencil, 2, 0) - derivative(stencil, 0, 2), derivative(stencil, 0, 1) - derivative(stencil, 1, 0)])


def conv_all(field, index_table, weights, biases, group_size, tables):
    row_count = field.shape[1]
    out_count = weights.shape[2]
    face_pool = jnp.take(field, tables[3], axis=2)

    def one_group(first_row):
        block_x = lax.dynamic_slice_in_dim(field, first_row, group_size, 1)
        index_rows = lax.dynamic_slice_in_dim(index_table, first_row, group_size, 0)
        stencil = make_taps(block_x, neighbour_faces(face_pool, index_rows), tables)
        summed = jnp.einsum('tcgv,tco->ogv', stencil.astype(jnp.float32), weights.astype(jnp.float32)) + biases[:, None, None]
        return jax.nn.silu(summed).astype(jnp.bfloat16)

    first_rows = jnp.arange(row_count // group_size, dtype=jnp.int32) * group_size
    stacked = lax.map(one_group, first_rows)
    return stacked.transpose(1, 0, 2, 3).reshape(out_count, row_count, 512)


def reference(features, neighbours, octants, owners, coarse_field, enc_weight, enc_bias, coarse_weight, coarse_bias, dec_weight, dec_bias, psi_weight):
    tables = voxel_tables()
    face_index, pool_matrix, to_coarse, to_octants = tables[3], tables[4], tables[5], tables[6]
    channels = features.shape[0]
    encoded = conv_all(features, neighbours, enc_weight, enc_bias, B_DEV, tables)
    pooled = jnp.einsum('cbv,vq->cbq', encoded.astype(jnp.float32), jnp.asarray(pool_matrix, jnp.float32)).astype(jnp.bfloat16)
    child_slot = (jnp.arange(BLOCKS, dtype=jnp.int32) // 8) * 8 + octants
    arranged = jnp.zeros_like(pooled).at[:, child_slot].set(pooled)
    arranged = jnp.take(arranged.reshape(channels, COARSE, 512), to_coarse, axis=2)
    owner_flat = owners[:, 0]
    grouped = owner_flat.reshape(N_SPACE, CB)
    same_owner = grouped[:, :, None] == grouped[:, None, :]
    positions = jnp.arange(CB, dtype=jnp.int32)
    earlier = positions[None, :] < positions[:, None]
    slot_rank = jnp.sum((same_owner & earlier[None, :, :]).astype(jnp.int32), axis=2).reshape(COARSE)
    source = jnp.arange(COARSE, dtype=jnp.int32) // CB
    owner_global = (source // WINDOW) * WINDOW + owner_flat
    slot_rows = owner_global * OSLOTS + (source % WINDOW) * PAIR + slot_rank
    given_field = jnp.take(coarse_field, slot_rows, axis=1)
    coarse_in = (arranged.astype(jnp.float32) + given_field.astype(jnp.float32)).astype(jnp.bfloat16)
    no_neighbours = -jnp.ones((COARSE, 6), jnp.int32)
    coarse_out = conv_all(coarse_in, no_neighbours, coarse_weight, coarse_bias, CB, tables)
    returned = jnp.take(coarse_out, to_octants, axis=2).reshape(channels, BLOCKS, 64)
    returned = jnp.take(returned, child_slot, axis=1)
    upsampled = jnp.einsum('cbq,vq->cbv', returned.astype(jnp.float32), jnp.asarray(pool_matrix * 8.0, jnp.float32))
    decoder_in = (encoded.astype(jnp.float32) + upsampled).astype(jnp.bfloat16)
    decoded = conv_all(decoder_in, neighbours, dec_weight, dec_bias, B_DEV, tables)
    stream = jnp.einsum('cbv,cm->mbv', decoded.astype(jnp.float32), psi_weight.astype(jnp.float32)).astype(jnp.bfloat16)
    stream_faces = jnp.take(stream, face_index, axis=2)

    def curl_group(first_row):
        block_x = lax.dynamic_slice_in_dim(stream, first_row, B_DEV, 1)
        index_rows = lax.dynamic_slice_in_dim(neighbours, first_row, B_DEV, 0)
        return curl_field(make_taps(block_x, neighbour_faces(stream_faces, index_rows), tables))

    first_rows = jnp.arange(N_SPACE, dtype=jnp.int32) * B_DEV
    stacked = lax.map(curl_group, first_rows)
    return stacked.transpose(1, 0, 2, 3).reshape(3, BLOCKS, 512)
```

```python
import functools

import jax
import jax.numpy as jnp
from jax import lax
from jax.experimental import pallas as pl
from jax.experimental.pallas import tpu as pltpu
from jax.sharding import PartitionSpec as P

BF = jnp.bfloat16
F32 = jnp.float32
WINDOW = 16
ABSENT = 40
NT = (((1,), (1,)), ((), ()))


def iota(shape, dim):
    return lax.broadcasted_iota(jnp.int32, shape, dim)


def dot(a, b):
    return jnp.dot(a, b, preferred_element_type=F32)


def shifts(own, nb):
    lane = iota(own[0].shape, 1)
    low, j, k = lane < 64, (lane >> 3) & 7, lane & 7
    turn = lambda x, steps: pltpu.roll(x, steps, 1)
    half = [turn(x, 64) for x in own]
    minus, plus = turn(nb(0, 3), 64), turn(nb(1, 0), 64)
    four = range(4)
    return [
        [jnp.where(low, half[q - 1] if q else minus, half[q]) for q in four],
        [jnp.where(low, half[q], half[q + 1] if q < 3 else plus) for q in four],
        [jnp.where(j == 0, turn(nb(2, q), 72), turn(own[q], 8)) for q in four],
        [jnp.where(j == 7, turn(nb(3, q), 56), turn(own[q], 120)) for q in four],
        [jnp.where(k == 0, turn(nb(4, q), 121), turn(own[q], 1)) for q in four],
        [jnp.where(k == 7, turn(nb(5, q), 7), turn(own[q], 127)) for q in four],
    ]


def quarters(x):
    return [x[:, 128 * q : 128 * q + 128] for q in range(4)]


def conv(own, nb, weight, bias):
    fields = [own] + shifts(own, nb)
    taps = jnp.concatenate([jnp.concatenate(f, axis=1) for f in fields], axis=0)
    u = dot(weight, taps) + bias
    return (0.5 * u * (1.0 + jnp.tanh(0.5 * u))).astype(BF)


def kernel(
    feat, cfield, nb_s, nb_v, oct_s, own_s, ew, eb, cw, cb, dw, db, psi,
    vel,
    fv, cv, pool_e, near_e, ct, fr, fsel, fsend, enc, pooled, eup, pool_d, near_d, dec, sp,
    perm, pmat, umat, wt, bt, psib, inv,
    load_sem, ce_s, ce_r, fe_s, fe_r, aa_s, aa_r, fx_s, fx_r, cd_s, cd_r, fd_s, fd_r, st_s, st_r,
):
    s, h = lax.axis_index("space"), lax.axis_index("chan")
    count = lax.axis_size("space")
    pos = s % WINDOW
    base = s - pos
    other = (s, 1 - h)
    after, before = (s + 1) % count, (s + count - 1) % count
    ch = pl.ds(pl.multiple_of(16 * h, 16), 16)

    def send(src, dst, ssem, rsem, device):
        return pltpu.make_async_remote_copy(
            src_ref=src, dst_ref=dst, send_sem=ssem, recv_sem=rsem,
            device_id=device, device_id_type=pl.DeviceIdType.MESH,
        )

    load_f = pltpu.make_async_copy(feat, fv, load_sem.at[0])
    load_c = pltpu.make_async_copy(cfield, cv, load_sem.at[1])
    load_f.start()
    load_c.start()

    barrier = pltpu.get_barrier_semaphore()
    peers = [(base + (pos + o) % WINDOW, h) for o in range(1, WINDOW)]
    everyone = peers + [other, (after, 0), (after, 1), (before, 0), (before, 1)]
    for device in everyone:
        pl.semaphore_signal(barrier, inc=1, device_id=device, device_id_type=pl.DeviceIdType.MESH)

    r, q = iota((256, 256), 0), iota((256, 256), 1)
    perm[...] = (q == (r & 15) * 16 + (r >> 4)).astype(BF)

    def cell(v):
        return ((v >> 7) << 6) + (((v >> 4) & 3) << 3) + ((v >> 1) & 3)

    pmat[...] = jnp.where(cell(iota((512, 256), 0)) == iota((512, 256), 1), 0.125, 0.0).astype(BF)
    umat[...] = (iota((256, 512), 0) == cell(iota((256, 512), 1))).astype(BF)
    eye = (iota((32, 32), 0) == iota((32, 32), 1)).astype(BF)
    for n, (w, b) in enumerate(((ew, eb), (cw, cb), (dw, db))):
        flat = w[...].reshape(224, 32)
        wt[n] = lax.dot_general(eye, flat, NT, preferred_element_type=F32).astype(BF)
        spread = jnp.where(iota((32, 32), 0) == iota((32, 32), 1), b[...], 0.0)
        bt[n] = jnp.broadcast_to(jnp.sum(spread, axis=1, keepdims=True), (32, 128))
    rows, lanes = iota((48, 512), 0), iota((48, 512), 1)
    tile = (iota((32, 512), 0) == (iota((32, 512), 1) & 31)).astype(BF)
    wide = lax.dot_general(
        psi[...], tile, (((0,), (0,)), ((), ())), preferred_element_type=F32
    )
    pick = jnp.concatenate([jnp.broadcast_to(wide[m : m + 1], (16, 512)) for m in range(3)], axis=0)
    psib[...] = jnp.where((rows & 15) == (lanes >> 5), pick, 0.0).astype(BF)
    pool_e[ABSENT] = jnp.zeros((32, 512), BF)
    pool_d[ABSENT] = jnp.zeros((32, 512), BF)
    for kl in range(2):
        for o in range(8):
            found = jnp.int32(0)
            for child in range(8):
                hit = oct_s[16 * h + 8 * kl + child] == o
                found = jnp.where(hit, jnp.int32(8 * kl + child), found)
            inv[8 * kl + o] = found

    pl.semaphore_wait(barrier, len(everyone))

    load_f.wait()
    for g in range(2):
        part = fv[:, 16 * g : 16 * g + 16, :].reshape(256, 512)
        pool_e[16 * g : 16 * g + 16, ch, :] = dot(perm[...], part).astype(BF).reshape(16, 16, 512)
    face_up = send(pool_e.at[24:32, ch], near_e.at[:, ch], fe_s.at[0], fe_r.at[h], (after, 0))
    face_down = send(pool_e.at[0:8, ch], near_e.at[:, ch], fe_s.at[1], fe_r.at[h], (before, 1))
    both = send(pool_e.at[0:32, ch], pool_e.at[0:32, ch], ce_s, ce_r, other)
    face_up.start()
    face_down.start()
    both.start()

    load_c.wait()
    for g in range(2):
        part = cv[:, 16 * g : 16 * g + 16, :].reshape(256, 512)
        ct[16 * g : 16 * g + 16] = dot(perm[...], part).astype(BF).reshape(16, 16, 512)
    spread_out = []
    for o in range(1, WINDOW):
        to = (pos + o) % WINDOW
        copy = send(
            ct.at[pl.ds(2 * to, 2)], fr.at[pl.ds(2 * pos, 2)], aa_s.at[o], aa_r.at[o], (base + to, h)
        )
        copy.start()
        spread_out.append(copy)
    fr[pl.ds(2 * pos, 2)] = ct[pl.ds(2 * pos, 2)]

    def fine(pool, n, out, first):
        weight, bias = wt[n], bt[n][:, :1]

        def body(t, carry):
            local = first + t
            row = 16 * h + local

            def spot(d):
                at = nb_s[row, d]
                rel = at - 32 * s
                return jnp.where(at < 0, ABSENT, rel & 63)

            spots = [spot(d) for d in range(6)]
            nb = lambda d, q: pool[spots[d], :, 128 * q : 128 * q + 128]
            out[local] = conv(quarters(pool[row]), nb, weight, bias)
            return carry

        lax.fori_loop(0, 8, body, 0)

    def pool_half(first):
        rows = enc[pl.ds(first, 8)].reshape(256, 512)
        pooled[pl.ds(first, 8)] = dot(rows, pmat[...]).astype(BF).reshape(8, 32, 256)

    inner, edge = 8 * (1 - h), 8 * h
    near = pl.ds(32 + 24 * (1 - h), 8)
    both.wait_recv()
    fine(pool_e, 0, enc, inner)
    pool_half(inner)
    for c in range(2):
        chc = pl.ds(16 * c, 16)
        send(pool_e.at[24:32, chc], near_e.at[:, chc], fe_s.at[0], fe_r.at[c], (after, 0)).wait_recv()
    pool_e[near, :, :] = near_e[...]
    fine(pool_e, 0, enc, edge)
    pool_half(edge)

    for copy in spread_out:
        copy.wait_recv()
    ow = [own_s[n, 0] for n in range(4)]
    slot = []
    for n in range(4):
        rank = jnp.int32(0)
        for m in range(n):
            rank = rank + jnp.where(ow[m] == ow[n], 1, 0)
        slot.append(2 * ow[n] + rank)
    for kl in range(2):
        mine = jnp.where(h == 0, slot[kl], slot[2 + kl])
        theirs = jnp.where(h == 0, slot[2 + kl], slot[kl])
        fsend[kl] = fr[theirs]
        fsel[kl, ch, :] = fr[mine]
    swap = send(fsend, fsel.at[:, ch], fx_s, fx_r, other)
    swap.start()

    gathered = []
    for kl in range(2):
        acc = [None, None]
        for o in range(8):
            part = pooled[inv[8 * kl + o]]
            step = 32 * ((o >> 1) & 1) + 4 * (o & 1)
            part = pltpu.roll(part, step, 1) if step else part
            acc[o >> 2] = part if acc[o >> 2] is None else acc[o >> 2] + part
        gathered.append(jnp.concatenate(acc, axis=1))
    swap.wait_recv()
    nothing = jnp.zeros((32, 128), BF)
    for kl in range(2):
        cin = (gathered[kl].astype(F32) + fsel[kl].astype(F32)).astype(BF)
        cout = conv(quarters(cin), lambda d, q: nothing, wt[1], bt[1][:, :1])
        parts = []
        for o in range(8):
            part = cout[:, 256 * (o >> 2) : 256 * (o >> 2) + 256]
            step = 32 * ((o >> 1) & 1) + 4 * (o & 1)
            parts.append(pltpu.roll(part, 256 - step, 1) if step else part)
        up = dot(jnp.concatenate(parts, axis=0), umat[...])
        eup[8 * kl : 8 * kl + 8] = up.astype(BF).reshape(8, 32, 512)

    def decoder_in(first):
        def body(t, carry):
            local = first + t
            row = 16 * h + local
            up = eup[first + oct_s[row]]
            pool_d[row] = (enc[local].astype(F32) + up.astype(F32)).astype(BF)
            return carry

        lax.fori_loop(0, 8, body, 0)

    partner = ((s + 2 * h - 1 + count) % count, 1 - h)
    decoder_in(edge)
    edge_rows = pl.ds(16 * h + edge, 8)
    face_d = send(pool_d.at[edge_rows], near_d, fd_s, fd_r, partner)
    face_d.start()
    cross = [send(pool_d.at[edge_rows], pool_d.at[edge_rows], cd_s.at[0], cd_r.at[0], other)]
    cross[0].start()
    decoder_in(inner)
    inner_rows = pl.ds(16 * h + inner, 8)
    cross.append(send(pool_d.at[inner_rows], pool_d.at[inner_rows], cd_s.at[1], cd_r.at[1], other))
    cross[1].start()
    cross[0].wait_recv()
    cross[1].wait_recv()
    fine(pool_d, 2, dec, inner)
    face_d.wait_recv()
    pool_d[near, :, :] = near_d[...]
    fine(pool_d, 2, dec, edge)

    stream = dot(psib[...], dec[...].reshape(512, 512)).astype(BF).reshape(3, 16, 512)
    own_rows = pl.ds(pl.multiple_of(16 + 16 * h, 16), 16)
    sp[:, own_rows, :] = stream
    side = s + 2 * h - 1 + count
    far = pl.ds(pl.multiple_of(48 * (1 - h), 16), 16)
    outgoing = [send(sp.at[:, own_rows], sp.at[:, far], st_s.at[1 + c], st_r.at[2 - h], (side % count, c)) for c in range(2)]
    outgoing.append(send(sp.at[:, own_rows], sp.at[:, own_rows], st_s.at[0], st_r.at[0], other))
    for copy in outgoing:
        copy.start()
    hots = []
    for d in range(6):
        at = nb_v[:, d : d + 1]
        rel = jnp.where(at < 0, -1, at - 32 * s + 16)
        hots.append((iota((32, 64), 1) == rel).astype(BF))
    outgoing[2].wait_recv()
    for n in range(1, 3):
        send(sp.at[:, own_rows], sp.at[:, far], st_s.at[n], st_r.at[n], other).wait_recv()

    diff = {}
    for m in range(3):
        axes = [a for a in range(3) if a != m]
        hot = jnp.concatenate([hots[2 * a + side_] for a in axes for side_ in range(2)], axis=0)
        faces = dot(hot, sp[m])
        own = quarters(sp[m, 16:48].astype(F32))
        pieces = {2 * a + e: quarters(faces[64 * n + 32 * e : 64 * n + 32 * e + 32]) for n, a in enumerate(axes) for e in range(2)}
        got = shifts(own, lambda d, q: pieces[d][q] if d in pieces else own[q])
        for a in axes:
            diff[a, m] = [0.5 * (x - y) for x, y in zip(got[2 * a + 1], got[2 * a])]
    for m in range(3):
        a, b = (m + 1) % 3, (m + 2) % 3
        vel[m] = jnp.concatenate([x - y for x, y in zip(diff[a, b], diff[b, a])], axis=1)

    face_up.wait_send()
    face_down.wait_send()
    both.wait_send()
    for copy in spread_out:
        copy.wait_send()
    swap.wait_send()
    face_d.wait_send()
    for copy in cross + outgoing:
        copy.wait_send()


def on_device(features, neighbours, octants, owners, coarse_field, ew, eb, cw, cb, dw, db, psi):
    vmem = pl.BlockSpec(memory_space=pltpu.VMEM)
    smem = pl.BlockSpec(memory_space=pltpu.SMEM)
    hbm = pl.BlockSpec(memory_space=pl.ANY)
    dma = pltpu.SemaphoreType.DMA
    v = lambda *shape: pltpu.VMEM(shape, BF)
    return pl.pallas_call(
        kernel,
        out_shape=jax.ShapeDtypeStruct((3, 32, 512), F32),
        in_specs=[hbm, hbm, smem, vmem, smem, smem] + [vmem] * 7,
        out_specs=vmem,
        scratch_shapes=[
            v(16, 32, 512), v(16, 32, 512), v(64, 32, 512), v(8, 32, 512),
            v(32, 16, 512), v(32, 16, 512), v(2, 32, 512), v(2, 16, 512),
            v(16, 32, 512), v(16, 32, 256), v(16, 32, 512), v(64, 32, 512), v(8, 32, 512),
            v(16, 32, 512), v(3, 64, 512),
            v(256, 256), v(512, 256), v(256, 512), v(3, 32, 224), pltpu.VMEM((3, 32, 128), F32),
            v(48, 512), pltpu.SMEM((16,), jnp.int32),
            dma((2,)), dma, dma, dma((2,)), dma((2,)), dma((16,)), dma((16,)), dma, dma,
            dma((2,)), dma((2,)), dma, dma, dma((3,)), dma((3,)),
        ],
        compiler_params=pltpu.CompilerParams(
            collective_id=0, has_side_effects=True, vmem_limit_bytes=48 * 1024 * 1024
        ),
    )(
        features, coarse_field, neighbours, neighbours, octants, owners,
        ew, eb.reshape(1, 32), cw, cb.reshape(1, 32), dw, db.reshape(1, 32), psi,
    )


def solution(mesh):
    split, rows = P("chan", "space", None), P("space", None)
    return jax.shard_map(
        on_device,
        mesh=mesh,
        in_specs=(split, rows, P("space"), rows, split) + (P(),) * 7,
        out_specs=P(None, "space", None),
        check_vma=False,
    )
```

```python
import jax
import jax.numpy as jnp
import numpy as np
from jax import lax
from jax.experimental import pallas as pl
from jax.experimental.pallas import tpu as pltpu
from jax.sharding import PartitionSpec as P

BF = jnp.bfloat16
F32 = jnp.float32
WINDOW = 16
ABSENT = 40
NT = (((1,), (1,)), ((), ()))


def tables():
    r = np.arange(256)
    perm = (r[:, None] % 16 * 16 + r[:, None] // 16 == r[None]).astype(np.float32)
    v = np.arange(512)
    i, j, k = v // 64, v // 8 % 8, v % 8
    cell = i // 2 * 64 + j // 2 * 8 + k // 2
    place = (cell[:, None] == r[None]).astype(np.float32)
    faces = np.zeros((2, 512, 256), np.float32)
    for n, end in enumerate((0, 7)):
        on_i, on_j, on_k = i == end, j == end, k == end
        faces[n, v[on_i], (j * 8 + k)[on_i]] = 1
        on_j &= ~on_i
        faces[n, v[on_j], 64 + (i * 8 + k)[on_j]] = 1
        on_k &= ~(i == end) & ~(j == end)
        faces[n, v[on_k], 128 + (i * 8 + j)[on_k]] = 1
    return [jnp.asarray(m, BF) for m in (perm, 0.125 * place, place.T, faces)]


def iota(shape, dim):
    return lax.broadcasted_iota(jnp.int32, shape, dim)


def dot(a, b):
    return jnp.dot(a, b, preferred_element_type=F32)


def shifts(own, nb):
    lane = iota(own[0].shape, 1)
    low, j, k = lane < 64, (lane >> 3) & 7, lane & 7
    turn = lambda x, steps: pltpu.roll(x, steps, 1)
    half = [turn(x, 64) for x in own]
    minus, plus = turn(nb(0, 3), 64), turn(nb(1, 0), 64)
    four = range(4)
    return [
        [jnp.where(low, half[q - 1] if q else minus, half[q]) for q in four],
        [jnp.where(low, half[q], half[q + 1] if q < 3 else plus) for q in four],
        [jnp.where(j == 0, turn(nb(2, q), 72), turn(own[q], 8)) for q in four],
        [jnp.where(j == 7, turn(nb(3, q), 56), turn(own[q], 120)) for q in four],
        [jnp.where(k == 0, turn(nb(4, q), 121), turn(own[q], 1)) for q in four],
        [jnp.where(k == 7, turn(nb(5, q), 7), turn(own[q], 127)) for q in four],
    ]


def quarters(x):
    return [x[:, 128 * q : 128 * q + 128] for q in range(4)]


def conv(own, nb, weight, bias):
    fields = [own] + shifts(own, nb)
    taps = jnp.concatenate([jnp.concatenate(f, axis=1) for f in fields], axis=0)
    u = dot(weight, taps) + bias
    return (0.5 * u * (1.0 + jnp.tanh(0.5 * u))).astype(BF)


def kernel(
    feat, cfield, nb_h, oct_h, own_h, ew_h, eb_h, cw_h, cb_h, dw_h, db_h, psi_h,
    perm_h, pmat_h, umat_h, face_h,
    vel_h,
    nb_s, oct_s, own_s, nb_v, ew, eb, cw, cb, dw, db, psi, vel, fv, cv, pool_e, pe, qe, ct, fr, fsel, fsend, enc, pooled, eup, pool_d, pd, qd, dec, sp, edge_s, far_s,
    perm, pmat, umat, faces, wt, bt, psib, psie, hots, inv,
    load_sem, out_sem, ce_s, ce_r, fe_s, fe_r, aa_s, aa_r, fx_s, fx_r, cd_s, cd_r, fd_s, fd_r, st_s, st_r,
):
    s, h = lax.axis_index("space"), lax.axis_index("chan")
    count = lax.axis_size("space")
    pos = s % WINDOW
    base = s - pos
    other = (s, 1 - h)
    after, before = s + 1, s - 1
    has_before, has_after = s > 0, s < count - 1
    has_near = jnp.where(h == 0, s, count - 1 - s) > 0
    ch = pl.ds(pl.multiple_of(16 * h, 16), 16)

    def send(src, dst, ssem, rsem, device):
        return pltpu.make_async_remote_copy(
            src_ref=src, dst_ref=dst, send_sem=ssem, recv_sem=rsem,
            device_id=device, device_id_type=pl.DeviceIdType.MESH,
        )

    load_f = pltpu.make_async_copy(feat, fv, load_sem.at[0])
    load_c = pltpu.make_async_copy(cfield, cv, load_sem.at[1])
    load_p = pltpu.make_async_copy(perm_h, perm, load_sem.at[15])
    load_q = pltpu.make_async_copy(face_h, faces, load_sem.at[16])
    for copy in (load_f, load_p, load_q, load_c):
        copy.start()
    ends = (
        (nb_h, nb_s), (oct_h, oct_s), (own_h, own_s), (nb_h, nb_v), (ew_h, ew), (eb_h, eb),
        (cw_h, cw), (cb_h, cb), (dw_h, dw), (db_h, db), (psi_h, psi), (pmat_h, pmat), (umat_h, umat),
    )
    small = [pltpu.make_async_copy(a, b, load_sem.at[2 + n]) for n, (a, b) in enumerate(ends)]
    for copy in small:
        copy.start()

    barrier = pltpu.get_barrier_semaphore()
    peers = [(base + (pos + o) % WINDOW, h) for o in range(1, WINDOW)]
    def greet(device):
        pl.semaphore_signal(barrier, inc=1, device_id=device, device_id_type=pl.DeviceIdType.MESH)

    for device in peers + [other]:
        greet(device)

    @pl.when(has_before)
    def _():
        greet((before, 0))
        greet((before, 1))

    @pl.when(has_after)
    def _():
        greet((after, 0))
        greet((after, 1))

    def pack(rows, which, out):
        width = rows.shape[1]
        got = dot(rows.reshape(8 * width, 512), faces[which]).astype(BF).reshape(8, width, 256)
        out[0:8] = got[:, :, :128]
        for b in range(4):
            lane = iota((width, 128), 1)
            out[8 + b] = jnp.where(lane < 64, got[b, :, 128:], pltpu.roll(got[4 + b, :, 128:], 64, 1))

    def unpack(got, which, pool):
        right = [got[8 + b] for b in range(4)]
        right = right + [pltpu.roll(x, 64, 1) for x in right]
        wide = jnp.concatenate([got[0:8].reshape(256, 128), jnp.concatenate(right, axis=0)], axis=1)
        full = lax.dot_general(wide, faces[which], NT, preferred_element_type=F32)
        pool[near, :, :] = full.astype(BF).reshape(8, 32, 512)

    inner, edge = 8 * (1 - h), 8 * h
    near = pl.ds(32 + 24 * (1 - h), 8)

    load_f.wait()
    load_p.wait()
    for g in range(2):
        part = fv[:, 16 * g : 16 * g + 16, :].reshape(256, 512)
        pool_e[16 * g : 16 * g + 16, ch, :] = dot(perm[...], part).astype(BF).reshape(16, 16, 512)
    load_q.wait()
    pack(pool_e[24:32, ch, :], 1, pe.at[1])
    pack(pool_e[0:8, ch, :], 0, pe.at[0])
    load_c.wait()
    for g in range(2):
        part = cv[:, 16 * g : 16 * g + 16, :].reshape(256, 512)
        ct[16 * g : 16 * g + 16] = dot(perm[...], part).astype(BF).reshape(16, 16, 512)
    extra = jnp.where(has_before, 2, 0) + jnp.where(has_after, 2, 0)
    pl.semaphore_wait(barrier, WINDOW + extra)

    face_up = send(pe.at[1], qe.at[:, ch], fe_s.at[0], fe_r.at[h], (after, 0))
    face_down = send(pe.at[0], qe.at[:, ch], fe_s.at[1], fe_r.at[h], (before, 1))
    both = send(pool_e.at[0:32, ch], pool_e.at[0:32, ch], ce_s, ce_r, other)
    pl.when(has_after)(face_up.start)
    pl.when(has_before)(face_down.start)
    spread_out = []
    for o in range(1, WINDOW):
        to = (pos + o) % WINDOW
        copy = send(
            ct.at[pl.ds(2 * to, 2)], fr.at[pl.ds(2 * pos, 2)], aa_s.at[o], aa_r.at[o], (base + to, h)
        )
        copy.start()
        spread_out.append(copy)
    both.start()
    fr[pl.ds(2 * pos, 2)] = ct[pl.ds(2 * pos, 2)]

    for copy in small:
        copy.wait()
    eye = (iota((32, 32), 0) == iota((32, 32), 1)).astype(BF)
    for n, (w, b) in enumerate(((ew, eb), (cw, cb), (dw, db))):
        flat = w[...].reshape(224, 32)
        wt[n] = lax.dot_general(eye, flat, NT, preferred_element_type=F32).astype(BF)
        spread = jnp.where(iota((32, 32), 0) == iota((32, 32), 1), b[...], 0.0)
        bt[n] = jnp.broadcast_to(jnp.sum(spread, axis=1, keepdims=True), (32, 128))
    tile = (iota((32, 512), 0) == (iota((32, 512), 1) & 31)).astype(BF)
    wide = dot(psi[...], tile)
    for out, width, used in ((psib, 16, 48), (psie, 8, 24)):
        size = out.shape
        pick = [jnp.broadcast_to(wide[m : m + 1, : size[1]], (width, size[1])) for m in range(3)]
        if used < size[0]:
            pick.append(jnp.zeros((size[0] - used, size[1]), F32))
        same = (iota(size, 0) & (width - 1)) == (iota(size, 1) >> 5)
        out[...] = jnp.where(same, jnp.concatenate(pick, axis=0), 0.0).astype(BF)
    pool_e[ABSENT] = jnp.zeros((32, 512), BF)
    pool_d[ABSENT] = jnp.zeros((32, 512), BF)
    at = nb_v[...]
    rel = jnp.where(at < 0, -1, at - 32 * s + 8).astype(F32).astype(BF)
    rel = lax.dot_general(eye, rel, NT, preferred_element_type=F32)
    place = iota((32, 48), 1).astype(F32)
    for d in range(6):
        hots[d] = (place == rel[:, d : d + 1]).astype(BF)
    for kl in range(2):
        for o in range(8):
            found = jnp.int32(0)
            for child in range(8):
                hit = oct_s[16 * h + 8 * kl + child] == o
                found = jnp.where(hit, jnp.int32(8 * kl + child), found)
            inv[8 * kl + o] = found

    def fine(pool, n, out, first):
        weight, bias = wt[n], bt[n][:, :1]

        def body(t, carry):
            local = first + t
            row = 16 * h + local

            def spot(d):
                at = nb_s[d, row]
                rel = at - 32 * s
                return jnp.where(at < 0, ABSENT, rel & 63)

            spots = [spot(d) for d in range(6)]
            nb = lambda d, q: pool[spots[d], :, 128 * q : 128 * q + 128]
            out[local] = conv(quarters(pool[row]), nb, weight, bias)
            return carry

        lax.fori_loop(0, 8, body, 0)

    def pool_half(first):
        rows = enc[pl.ds(first, 8)].reshape(256, 512)
        pooled[pl.ds(first, 8)] = dot(rows, pmat[...]).astype(BF).reshape(8, 32, 256)

    both.wait_recv()
    fine(pool_e, 0, enc, inner)
    pool_half(inner)
    @pl.when(has_near)
    def _():
        for c in range(2):
            chc = pl.ds(16 * c, 16)
            send(pe.at[0], qe.at[:, chc], fe_s.at[0], fe_r.at[c], (s, 1 - h)).wait_recv()
        unpack(qe, 1 - h, pool_e)

    fine(pool_e, 0, enc, edge)
    pool_half(edge)

    for copy in spread_out:
        copy.wait_recv()
    ow = [own_s[0, n] for n in range(4)]
    slot = []
    for n in range(4):
        rank = jnp.int32(0)
        for m in range(n):
            rank = rank + jnp.where(ow[m] == ow[n], 1, 0)
        slot.append(2 * ow[n] + rank)
    for kl in range(2):
        mine = jnp.where(h == 0, slot[kl], slot[2 + kl])
        theirs = jnp.where(h == 0, slot[2 + kl], slot[kl])
        fsend[kl] = fr[theirs]
        fsel[kl, ch, :] = fr[mine]
    swap = send(fsend, fsel.at[:, ch], fx_s, fx_r, other)
    swap.start()

    def gather(kl):
        acc = [None, None]
        for o in range(8):
            part = pooled[inv[8 * kl + o]]
            step = 32 * ((o >> 1) & 1) + 4 * (o & 1)
            part = pltpu.roll(part, step, 1) if step else part
            acc[o >> 2] = part if acc[o >> 2] is None else acc[o >> 2] + part
        return jnp.concatenate(acc, axis=1)

    gathered = [gather(h), gather(1 - h)]
    swap.wait_recv()
    nothing = jnp.zeros((32, 128), BF)

    def coarse(kl, children):
        cin = (children.astype(F32) + fsel[kl].astype(F32)).astype(BF)
        cout = conv(quarters(cin), lambda d, q: nothing, wt[1], bt[1][:, :1])
        parts = []
        for o in range(8):
            part = cout[:, 256 * (o >> 2) : 256 * (o >> 2) + 256]
            step = 32 * ((o >> 1) & 1) + 4 * (o & 1)
            parts.append(pltpu.roll(part, 256 - step, 1) if step else part)
        up = dot(jnp.concatenate(parts, axis=0), umat[...])
        eup[pl.ds(8 * kl, 8)] = up.astype(BF).reshape(8, 32, 512)

    def decoder_in(first):
        def body(t, carry):
            local = first + t
            row = 16 * h + local
            up = eup[first + oct_s[row]]
            pool_d[row] = (enc[local].astype(F32) + up.astype(F32)).astype(BF)
            return carry

        lax.fori_loop(0, 8, body, 0)

    partner = (s + 2 * h - 1, 1 - h)
    coarse(h, gathered[0])
    decoder_in(edge)
    edge_rows = pl.ds(16 * h + edge, 8)
    pack(pool_d[edge_rows], h, pd)
    face_d = send(pd, qd, fd_s, fd_r, partner)
    pl.when(has_near)(face_d.start)
    cross = [send(pool_d.at[edge_rows], pool_d.at[edge_rows], cd_s.at[0], cd_r.at[0], other)]
    cross[0].start()
    coarse(1 - h, gathered[1])
    decoder_in(inner)
    inner_rows = pl.ds(16 * h + inner, 8)
    cross.append(send(pool_d.at[inner_rows], pool_d.at[inner_rows], cd_s.at[1], cd_r.at[1], other))
    cross[1].start()
    cross[0].wait_recv()
    cross[1].wait_recv()
    fine(pool_d, 2, dec, inner)

    @pl.when(has_near)
    def _():
        face_d.wait_recv()
        unpack(qd, 1 - h, pool_d)

    fine(pool_d, 2, dec, edge)

    edge_s[...] = dot(psie[...], dec[pl.ds(edge, 8)].reshape(256, 512)).astype(BF)
    side = s + 2 * h - 1
    far = [send(edge_s, far_s.at[1 - h], st_s.at[1 + c], st_r.at[2 - h], (side, c)) for c in range(2)]
    for copy in far:
        pl.when(has_near)(copy.start)
    own_rows = pl.ds(pl.multiple_of(16 * h, 16), 16)
    sp[:, own_rows, :] = dot(psib[...], dec[...].reshape(512, 512)).astype(BF).reshape(3, 16, 512)
    beside = send(sp.at[:, own_rows], sp.at[:, own_rows], st_s.at[0], st_r.at[0], other)
    beside.start()
    beside.wait_recv()
    for n, there in ((0, has_before), (1, has_after)):

        @pl.when(there)
        def _():
            send(edge_s, far_s.at[n], st_s.at[1], st_r.at[1 + n], other).wait_recv()

        @pl.when(jnp.logical_not(there))
        def _():
            far_s[n] = jnp.zeros((32, 512), BF)

    diff = {}
    for m in range(3):
        axes = [a for a in range(3) if a != m]
        hot = jnp.concatenate([hots[2 * a + side_] for a in axes for side_ in range(2)], axis=0)
        mine = sp[m].astype(F32)
        lower, upper = (far_s[n].astype(F32)[8 * m : 8 * m + 8] for n in range(2))
        near_faces = dot(hot, jnp.concatenate([lower, mine, upper], axis=0).astype(BF))
        own = quarters(mine)
        pieces = {2 * a + e: quarters(near_faces[64 * n + 32 * e : 64 * n + 32 * e + 32]) for n, a in enumerate(axes) for e in range(2)}
        got = shifts(own, lambda d, q: pieces[d][q] if d in pieces else own[q])
        for a in axes:
            diff[a, m] = [0.5 * (x - y) for x, y in zip(got[2 * a + 1], got[2 * a])]
    for m in range(3):
        a, b = (m + 1) % 3, (m + 2) % 3
        vel[m] = jnp.concatenate([x - y for x, y in zip(diff[a, b], diff[b, a])], axis=1)
    store = pltpu.make_async_copy(vel, vel_h, out_sem)
    store.start()

    pl.when(has_after)(face_up.wait_send)
    pl.when(has_before)(face_down.wait_send)
    for copy in spread_out + cross + [both, swap, beside]:
        copy.wait_send()
    for copy in [face_d] + far:
        pl.when(has_near)(copy.wait_send)
    store.wait()


def on_device(features, neighbours, octants, owners, coarse_field, ew, eb, cw, cb, dw, db, psi):
    hbm = pl.BlockSpec(memory_space=pltpu.HBM)
    dma = pltpu.SemaphoreType.DMA
    v = lambda *shape: pltpu.VMEM(shape, BF)
    f = lambda *shape: pltpu.VMEM(shape, F32)
    return pl.pallas_call(
        kernel,
        out_shape=jax.ShapeDtypeStruct((3, 32, 512), F32),
        in_specs=[hbm] * 16,
        out_specs=hbm,
        scratch_shapes=[
            pltpu.SMEM((6, 32), jnp.int32), pltpu.SMEM((32,), jnp.int32), pltpu.SMEM((1, 4), jnp.int32),
            pltpu.VMEM((6, 32), jnp.int32), v(7, 32, 32), f(1, 32), v(7, 32, 32), f(1, 32),
            v(7, 32, 32), f(1, 32), v(3, 32), f(3, 32, 512),
            v(16, 32, 512), v(16, 32, 512), v(64, 32, 512), v(2, 12, 16, 128), v(12, 32, 128),
            v(32, 16, 512), v(32, 16, 512), v(2, 32, 512), v(2, 16, 512),
            v(16, 32, 512), v(16, 32, 256), v(16, 32, 512), v(64, 32, 512), v(12, 32, 128), v(12, 32, 128),
            v(16, 32, 512), v(3, 32, 512), v(32, 512), v(2, 32, 512),
            v(256, 256), v(512, 256), v(256, 512), v(2, 512, 256), v(3, 32, 224), pltpu.VMEM((3, 32, 128), F32),
            v(48, 512), v(32, 256), v(6, 32, 48), pltpu.SMEM((16,), jnp.int32),
            dma((17,)), dma, dma, dma, dma((2,)), dma((2,)), dma((16,)), dma((16,)), dma, dma,
            dma((2,)), dma((2,)), dma, dma, dma((3,)), dma((3,)),
        ],
        compiler_params=pltpu.CompilerParams(
            collective_id=0, has_side_effects=True, vmem_limit_bytes=63 * 1024 * 1024
        ),
    )(
        features, coarse_field, neighbours.T, octants, owners.reshape(1, 4),
        ew, eb.reshape(1, 32), cw, cb.reshape(1, 32), dw, db.reshape(1, 32), psi.T, *tables(),
    )


def solution(mesh):
    split, rows = P("chan", "space", None), P("space", None)
    return jax.shard_map(
        on_device,
        mesh=mesh,
        in_specs=(split, rows, P("space"), rows, split) + (P(),) * 7,
        out_specs=P(None, "space", None),
        check_vma=False,
    )
```

```python
import jax
import jax.numpy as jnp
import numpy as np
from jax import lax
from jax.experimental import pallas as pl
from jax.experimental.pallas import tpu as pltpu
from jax.sharding import PartitionSpec as P

BF = jnp.bfloat16
F32 = jnp.float32
WINDOW = 16
ABSENT = 40
NT = (((1,), (1,)), ((), ()))


def tables():
    r = np.arange(256)
    perm = (r[:, None] % 16 * 16 + r[:, None] // 16 == r[None]).astype(np.float32)
    v = np.arange(512)
    i, j, k = v // 64, v // 8 % 8, v % 8
    cell = i // 2 * 64 + j // 2 * 8 + k // 2
    place = (cell[:, None] == r[None]).astype(np.float32)
    faces = np.zeros((2, 512, 256), np.float32)
    for n, end in enumerate((0, 7)):
        on_i, on_j, on_k = i == end, j == end, k == end
        faces[n, v[on_i], (j * 8 + k)[on_i]] = 1
        on_j &= ~on_i
        faces[n, v[on_j], 64 + (i * 8 + k)[on_j]] = 1
        on_k &= ~(i == end) & ~(j == end)
        faces[n, v[on_k], 128 + (i * 8 + j)[on_k]] = 1
    return [jnp.asarray(m, BF) for m in (perm, 0.125 * place, place.T, faces)]


def iota(shape, dim):
    return lax.broadcasted_iota(jnp.int32, shape, dim)


def dot(a, b):
    return jnp.dot(a, b, preferred_element_type=F32)


def shifts(own, nb):
    lane = iota(own[0].shape, 1)
    low, j, k = lane < 64, (lane >> 3) & 7, lane & 7
    turn = lambda x, steps: pltpu.roll(x, steps, 1)
    half = [turn(x, 64) for x in own]
    minus, plus = turn(nb(0, 3), 64), turn(nb(1, 0), 64)
    four = range(4)
    return [
        [jnp.where(low, half[q - 1] if q else minus, half[q]) for q in four],
        [jnp.where(low, half[q], half[q + 1] if q < 3 else plus) for q in four],
        [jnp.where(j == 0, turn(nb(2, q), 72), turn(own[q], 8)) for q in four],
        [jnp.where(j == 7, turn(nb(3, q), 56), turn(own[q], 120)) for q in four],
        [jnp.where(k == 0, turn(nb(4, q), 121), turn(own[q], 1)) for q in four],
        [jnp.where(k == 7, turn(nb(5, q), 7), turn(own[q], 127)) for q in four],
    ]


def quarters(x):
    return [x[:, 128 * q : 128 * q + 128] for q in range(4)]


def conv(own, nb, weight, bias):
    fields = [own] + shifts(own, nb)
    taps = jnp.concatenate([jnp.concatenate(f, axis=1) for f in fields], axis=0)
    u = dot(weight, taps) + bias
    return (0.5 * u * (1.0 + jnp.tanh(0.5 * u))).astype(BF)


def kernel(
    feat, cfield, nb_h, oct_h, own_h, ew_h, eb_h, cw_h, cb_h, dw_h, db_h, psi_h,
    perm_h, pmat_h, umat_h, face_h,
    vel_h,
    nb_s, oct_s, own_s, nb_v, ew, eb, cw, cb, dw, db, psi, vel, fv, cv, pool_e, pe, qe, ct, fr, fsel, fsend, enc, pooled, eup, pool_d, pd, qd, dec, sp, edge_s, far_s,
    perm, pmat, umat, faces, wt, bt, psib, psie, hots, inv,
    load_sem, out_sem, ce_s, ce_r, fe_s, fe_r, aa_s, aa_r, fx_s, fx_r, cd_s, cd_r, fd_s, fd_r, st_s, st_r,
):
    s, h = lax.axis_index("space"), lax.axis_index("chan")
    count = lax.axis_size("space")
    pos = s % WINDOW
    base = s - pos
    other = (s, 1 - h)
    after, before = s + 1, s - 1
    has_before, has_after = s > 0, s < count - 1
    has_near = jnp.where(h == 0, s, count - 1 - s) > 0
    ch = pl.ds(pl.multiple_of(16 * h, 16), 16)

    def send(src, dst, ssem, rsem, device):
        return pltpu.make_async_remote_copy(
            src_ref=src, dst_ref=dst, send_sem=ssem, recv_sem=rsem,
            device_id=device, device_id_type=pl.DeviceIdType.MESH,
        )

    barrier = pltpu.get_barrier_semaphore()
    peers = [(base + (pos + o) % WINDOW, h) for o in range(1, WINDOW)]
    def greet(device):
        pl.semaphore_signal(barrier, inc=1, device_id=device, device_id_type=pl.DeviceIdType.MESH)

    for device in peers + [other]:
        greet(device)

    @pl.when(has_before)
    def _():
        greet((before, 0))
        greet((before, 1))

    @pl.when(has_after)
    def _():
        greet((after, 0))
        greet((after, 1))

    load_f = pltpu.make_async_copy(feat, fv, load_sem.at[0])
    load_c = pltpu.make_async_copy(cfield, cv, load_sem.at[1])
    load_p = pltpu.make_async_copy(perm_h, perm, load_sem.at[15])
    load_q = pltpu.make_async_copy(face_h, faces, load_sem.at[16])
    for copy in (load_f, load_p, load_q, load_c):
        copy.start()

    def pack(rows, which, out):
        width = rows.shape[1]
        got = dot(rows.reshape(8 * width, 512), faces[which]).astype(BF).reshape(8, width, 256)
        out[0:8] = got[:, :, :128]
        for b in range(4):
            lane = iota((width, 128), 1)
            out[8 + b] = jnp.where(lane < 64, got[b, :, 128:], pltpu.roll(got[4 + b, :, 128:], 64, 1))

    def unpack(got, which, pool):
        right = [got[8 + b] for b in range(4)]
        right = right + [pltpu.roll(x, 64, 1) for x in right]
        wide = jnp.concatenate([got[0:8].reshape(256, 128), jnp.concatenate(right, axis=0)], axis=1)
        full = lax.dot_general(wide, faces[which], NT, preferred_element_type=F32)
        pool[near, :, :] = full.astype(BF).reshape(8, 32, 512)

    inner, edge = 8 * (1 - h), 8 * h
    near = pl.ds(32 + 24 * (1 - h), 8)

    ends = (
        (nb_h, nb_s), (oct_h, oct_s), (own_h, own_s), (nb_h, nb_v), (ew_h, ew), (eb_h, eb),
        (cw_h, cw), (cb_h, cb), (dw_h, dw), (db_h, db), (psi_h, psi), (pmat_h, pmat), (umat_h, umat),
    )
    small = [pltpu.make_async_copy(a, b, load_sem.at[2 + n]) for n, (a, b) in enumerate(ends)]
    for copy in small:
        copy.start()
    load_f.wait()
    load_p.wait()
    for g in range(2):
        part = fv[:, 16 * g : 16 * g + 16, :].reshape(256, 512)
        pool_e[16 * g : 16 * g + 16, ch, :] = dot(perm[...], part).astype(BF).reshape(16, 16, 512)
    load_q.wait()
    pack(pool_e[24:32, ch, :], 1, pe.at[1])
    pack(pool_e[0:8, ch, :], 0, pe.at[0])
    load_c.wait()
    for g in range(2):
        part = cv[:, 16 * g : 16 * g + 16, :].reshape(256, 512)
        ct[16 * g : 16 * g + 16] = dot(perm[...], part).astype(BF).reshape(16, 16, 512)
    extra = jnp.where(has_before, 2, 0) + jnp.where(has_after, 2, 0)
    pl.semaphore_wait(barrier, WINDOW + extra)

    face_up = send(pe.at[1], qe.at[:, ch], fe_s.at[0], fe_r.at[h], (after, 0))
    face_down = send(pe.at[0], qe.at[:, ch], fe_s.at[1], fe_r.at[h], (before, 1))
    both = send(pool_e.at[0:32, ch], pool_e.at[0:32, ch], ce_s, ce_r, other)
    pl.when(has_after)(face_up.start)
    pl.when(has_before)(face_down.start)
    spread_out = []
    for o in (1, 7, 8, 9, 15, 2, 6, 10, 14, 3, 5, 11, 13, 4, 12):
        to = (pos + o) % WINDOW
        copy = send(
            ct.at[pl.ds(2 * to, 2)], fr.at[pl.ds(2 * pos, 2)], aa_s.at[o], aa_r.at[o], (base + to, h)
        )
        copy.start()
        spread_out.append(copy)
    both.start()
    fr[pl.ds(2 * pos, 2)] = ct[pl.ds(2 * pos, 2)]

    for copy in small:
        copy.wait()
    eye = (iota((32, 32), 0) == iota((32, 32), 1)).astype(BF)
    for n, (w, b) in enumerate(((ew, eb), (cw, cb), (dw, db))):
        flat = w[...].reshape(224, 32)
        wt[n] = lax.dot_general(eye, flat, NT, preferred_element_type=F32).astype(BF)
        spread = jnp.where(iota((32, 32), 0) == iota((32, 32), 1), b[...], 0.0)
        bt[n] = jnp.broadcast_to(jnp.sum(spread, axis=1, keepdims=True), (32, 128))
    tile = (iota((32, 512), 0) == (iota((32, 512), 1) & 31)).astype(BF)
    wide = dot(psi[...], tile)
    for out, width, used in ((psib, 16, 48), (psie, 8, 24)):
        size = out.shape
        pick = [jnp.broadcast_to(wide[m : m + 1, : size[1]], (width, size[1])) for m in range(3)]
        if used < size[0]:
            pick.append(jnp.zeros((size[0] - used, size[1]), F32))
        same = (iota(size, 0) & (width - 1)) == (iota(size, 1) >> 5)
        out[...] = jnp.where(same, jnp.concatenate(pick, axis=0), 0.0).astype(BF)
    pool_e[ABSENT] = jnp.zeros((32, 512), BF)
    pool_d[ABSENT] = jnp.zeros((32, 512), BF)
    at = nb_v[...]
    rel = jnp.where(at < 0, -1, at - 32 * s + 8).astype(F32).astype(BF)
    rel = lax.dot_general(eye, rel, NT, preferred_element_type=F32)
    place = iota((32, 48), 1).astype(F32)
    for d in range(6):
        hots[d] = (place == rel[:, d : d + 1]).astype(BF)
    for kl in range(2):
        for o in range(8):
            found = jnp.int32(0)
            for child in range(8):
                hit = oct_s[16 * h + 8 * kl + child] == o
                found = jnp.where(hit, jnp.int32(8 * kl + child), found)
            inv[8 * kl + o] = found

    def fine(pool, n, out, first):
        weight, bias = wt[n], bt[n][:, :1]

        def body(t, carry):
            local = first + t
            row = 16 * h + local

            def spot(d):
                at = nb_s[d, row]
                rel = at - 32 * s
                return jnp.where(at < 0, ABSENT, rel & 63)

            spots = [spot(d) for d in range(6)]
            nb = lambda d, q: pool[spots[d], :, 128 * q : 128 * q + 128]
            out[local] = conv(quarters(pool[row]), nb, weight, bias)
            return carry

        lax.fori_loop(0, 8, body, 0, unroll=8)

    def pool_half(first):
        rows = enc[pl.ds(first, 8)].reshape(256, 512)
        pooled[pl.ds(first, 8)] = dot(rows, pmat[...]).astype(BF).reshape(8, 32, 256)

    both.wait_recv()
    fine(pool_e, 0, enc, inner)
    pool_half(inner)
    @pl.when(has_near)
    def _():
        for c in range(2):
            chc = pl.ds(16 * c, 16)
            send(pe.at[0], qe.at[:, chc], fe_s.at[0], fe_r.at[c], (s, 1 - h)).wait_recv()
        unpack(qe, 1 - h, pool_e)

    fine(pool_e, 0, enc, edge)
    pool_half(edge)

    for copy in spread_out:
        copy.wait_recv()
    ow = [own_s[0, n] for n in range(4)]
    slot = []
    for n in range(4):
        rank = jnp.int32(0)
        for m in range(n):
            rank = rank + jnp.where(ow[m] == ow[n], 1, 0)
        slot.append(2 * ow[n] + rank)
    for kl in range(2):
        mine = jnp.where(h == 0, slot[kl], slot[2 + kl])
        theirs = jnp.where(h == 0, slot[2 + kl], slot[kl])
        fsend[kl] = fr[theirs]
        fsel[kl, ch, :] = fr[mine]
    swap = send(fsend, fsel.at[:, ch], fx_s, fx_r, other)
    swap.start()

    def gather(kl):
        acc = [None, None]
        for o in range(8):
            part = pooled[inv[8 * kl + o]]
            step = 32 * ((o >> 1) & 1) + 4 * (o & 1)
            part = pltpu.roll(part, step, 1) if step else part
            acc[o >> 2] = part if acc[o >> 2] is None else acc[o >> 2] + part
        return jnp.concatenate(acc, axis=1)

    gathered = [gather(h), gather(1 - h)]
    swap.wait_recv()
    nothing = jnp.zeros((32, 128), BF)

    def coarse(kl, children):
        cin = (children.astype(F32) + fsel[kl].astype(F32)).astype(BF)
        cout = conv(quarters(cin), lambda d, q: nothing, wt[1], bt[1][:, :1])
        parts = []
        for o in range(8):
            part = cout[:, 256 * (o >> 2) : 256 * (o >> 2) + 256]
            step = 32 * ((o >> 1) & 1) + 4 * (o & 1)
            parts.append(pltpu.roll(part, 256 - step, 1) if step else part)
        up = dot(jnp.concatenate(parts, axis=0), umat[...])
        eup[pl.ds(8 * kl, 8)] = up.astype(BF).reshape(8, 32, 512)

    def decoder_in(first):
        def body(t, carry):
            local = first + t
            row = 16 * h + local
            up = eup[first + oct_s[row]]
            pool_d[row] = (enc[local].astype(F32) + up.astype(F32)).astype(BF)
            return carry

        lax.fori_loop(0, 8, body, 0, unroll=8)

    partner = (s + 2 * h - 1, 1 - h)
    coarse(h, gathered[0])
    decoder_in(edge)
    edge_rows = pl.ds(16 * h + edge, 8)
    pack(pool_d[edge_rows], h, pd)
    face_d = send(pd, qd, fd_s, fd_r, partner)
    pl.when(has_near)(face_d.start)
    cross = [send(pool_d.at[edge_rows], pool_d.at[edge_rows], cd_s.at[0], cd_r.at[0], other)]
    cross[0].start()
    coarse(1 - h, gathered[1])
    decoder_in(inner)
    inner_rows = pl.ds(16 * h + inner, 8)
    cross.append(send(pool_d.at[inner_rows], pool_d.at[inner_rows], cd_s.at[1], cd_r.at[1], other))
    cross[1].start()
    cross[0].wait_recv()
    cross[1].wait_recv()
    fine(pool_d, 2, dec, inner)

    @pl.when(has_near)
    def _():
        face_d.wait_recv()
        unpack(qd, 1 - h, pool_d)

    fine(pool_d, 2, dec, edge)

    edge_s[...] = dot(psie[...], dec[pl.ds(edge, 8)].reshape(256, 512)).astype(BF)
    side = s + 2 * h - 1
    far = [send(edge_s, far_s.at[1 - h], st_s.at[1 + c], st_r.at[2 - h], (side, c)) for c in range(2)]
    for copy in far:
        pl.when(has_near)(copy.start)
    own_rows = pl.ds(pl.multiple_of(16 * h, 16), 16)
    sp[:, own_rows, :] = dot(psib[...], dec[...].reshape(512, 512)).astype(BF).reshape(3, 16, 512)
    beside = send(sp.at[:, own_rows], sp.at[:, own_rows], st_s.at[0], st_r.at[0], other)
    beside.start()
    beside.wait_recv()
    for n, there in ((0, has_before), (1, has_after)):

        @pl.when(there)
        def _():
            send(edge_s, far_s.at[n], st_s.at[1], st_r.at[1 + n], other).wait_recv()

        @pl.when(jnp.logical_not(there))
        def _():
            far_s[n] = jnp.zeros((32, 512), BF)

    diff = {}
    for m in range(3):
        axes = [a for a in range(3) if a != m]
        hot = jnp.concatenate([hots[2 * a + side_] for a in axes for side_ in range(2)], axis=0)
        mine = sp[m].astype(F32)
        lower, upper = (far_s[n].astype(F32)[8 * m : 8 * m + 8] for n in range(2))
        near_faces = dot(hot, jnp.concatenate([lower, mine, upper], axis=0).astype(BF))
        own = quarters(mine)
        pieces = {2 * a + e: quarters(near_faces[64 * n + 32 * e : 64 * n + 32 * e + 32]) for n, a in enumerate(axes) for e in range(2)}
        got = shifts(own, lambda d, q: pieces[d][q] if d in pieces else own[q])
        for a in axes:
            diff[a, m] = [0.5 * (x - y) for x, y in zip(got[2 * a + 1], got[2 * a])]
    for m in range(3):
        a, b = (m + 1) % 3, (m + 2) % 3
        vel[m] = jnp.concatenate([x - y for x, y in zip(diff[a, b], diff[b, a])], axis=1)
    store = pltpu.make_async_copy(vel, vel_h, out_sem)
    store.start()

    pl.when(has_after)(face_up.wait_send)
    pl.when(has_before)(face_down.wait_send)
    for copy in spread_out + cross + [both, swap, beside]:
        copy.wait_send()
    for copy in [face_d] + far:
        pl.when(has_near)(copy.wait_send)
    store.wait()


def on_device(features, neighbours, octants, owners, coarse_field, ew, eb, cw, cb, dw, db, psi):
    hbm = pl.BlockSpec(memory_space=pltpu.HBM)
    dma = pltpu.SemaphoreType.DMA
    v = lambda *shape: pltpu.VMEM(shape, BF)
    f = lambda *shape: pltpu.VMEM(shape, F32)
    return pl.pallas_call(
        kernel,
        out_shape=jax.ShapeDtypeStruct((3, 32, 512), F32),
        in_specs=[hbm] * 16,
        out_specs=hbm,
        scratch_shapes=[
            pltpu.SMEM((6, 32), jnp.int32), pltpu.SMEM((32,), jnp.int32), pltpu.SMEM((1, 4), jnp.int32),
            pltpu.VMEM((6, 32), jnp.int32), v(7, 32, 32), f(1, 32), v(7, 32, 32), f(1, 32),
            v(7, 32, 32), f(1, 32), v(3, 32), f(3, 32, 512),
            v(16, 32, 512), v(16, 32, 512), v(64, 32, 512), v(2, 12, 16, 128), v(12, 32, 128),
            v(32, 16, 512), v(32, 16, 512), v(2, 32, 512), v(2, 16, 512),
            v(16, 32, 512), v(16, 32, 256), v(16, 32, 512), v(64, 32, 512), v(12, 32, 128), v(12, 32, 128),
            v(16, 32, 512), v(3, 32, 512), v(32, 512), v(2, 32, 512),
            v(256, 256), v(512, 256), v(256, 512), v(2, 512, 256), v(3, 32, 224), pltpu.VMEM((3, 32, 128), F32),
            v(48, 512), v(32, 256), v(6, 32, 48), pltpu.SMEM((16,), jnp.int32),
            dma((17,)), dma, dma, dma, dma((2,)), dma((2,)), dma((16,)), dma((16,)), dma, dma,
            dma((2,)), dma((2,)), dma, dma, dma((3,)), dma((3,)),
        ],
        compiler_params=pltpu.CompilerParams(
            collective_id=0, has_side_effects=True, vmem_limit_bytes=63 * 1024 * 1024
        ),
    )(
        features, coarse_field, neighbours.T, octants, owners.reshape(1, 4),
        ew, eb.reshape(1, 32), cw, cb.reshape(1, 32), dw, db.reshape(1, 32), psi.T, *tables(),
    )


def solution(mesh):
    split, rows = P("chan", "space", None), P("space", None)
    return jax.shard_map(
        on_device,
        mesh=mesh,
        in_specs=(split, rows, P("space"), rows, split) + (P(),) * 7,
        out_specs=P(None, "space", None),
        check_vma=False,
    )
```

```python
import jax
import jax.numpy as jnp
import numpy as np
from jax import lax
from jax.experimental import pallas as pl
from jax.experimental.pallas import tpu as pltpu
from jax.sharding import PartitionSpec as P

BF = jnp.bfloat16
F32 = jnp.float32
WINDOW = 16
ABSENT = 40
NT = (((1,), (1,)), ((), ()))


def tables():
    r = np.arange(256)
    perm = (r[:, None] % 16 * 16 + r[:, None] // 16 == r[None]).astype(np.float32)
    v = np.arange(512)
    i, j, k = v // 64, v // 8 % 8, v % 8
    cell = i // 2 * 64 + j // 2 * 8 + k // 2
    place = (cell[:, None] == r[None]).astype(np.float32)
    faces = np.zeros((2, 512, 256), np.float32)
    for n, end in enumerate((0, 7)):
        on_i, on_j, on_k = i == end, j == end, k == end
        faces[n, v[on_i], (j * 8 + k)[on_i]] = 1
        on_j &= ~on_i
        faces[n, v[on_j], 64 + (i * 8 + k)[on_j]] = 1
        on_k &= ~(i == end) & ~(j == end)
        faces[n, v[on_k], 128 + (i * 8 + j)[on_k]] = 1
    return [jnp.asarray(m, BF) for m in (perm, 0.125 * place, place.T, faces)]


def iota(shape, dim):
    return lax.broadcasted_iota(jnp.int32, shape, dim)


def dot(a, b):
    return jnp.dot(a, b, preferred_element_type=F32)


def shifts(own, nb):
    lane = iota(own[0].shape, 1)
    low, j, k = lane < 64, (lane >> 3) & 7, lane & 7
    turn = lambda x, steps: pltpu.roll(x, steps, 1)
    half = [turn(x, 64) for x in own]
    minus, plus = turn(nb(0, 3), 64), turn(nb(1, 0), 64)
    four = range(4)
    return [
        [jnp.where(low, half[q - 1] if q else minus, half[q]) for q in four],
        [jnp.where(low, half[q], half[q + 1] if q < 3 else plus) for q in four],
        [jnp.where(j == 0, turn(nb(2, q), 72), turn(own[q], 8)) for q in four],
        [jnp.where(j == 7, turn(nb(3, q), 56), turn(own[q], 120)) for q in four],
        [jnp.where(k == 0, turn(nb(4, q), 121), turn(own[q], 1)) for q in four],
        [jnp.where(k == 7, turn(nb(5, q), 7), turn(own[q], 127)) for q in four],
    ]


def quarters(x):
    return [x[:, 128 * q : 128 * q + 128] for q in range(4)]


def conv(own, nb, weight, bias):
    fields = [own] + shifts(own, nb)
    taps = jnp.concatenate([jnp.concatenate(f, axis=1) for f in fields], axis=0)
    u = dot(weight, taps) + bias
    return (0.5 * u * (1.0 + jnp.tanh(0.5 * u))).astype(BF)


def kernel(
    feat, cfield, nb_h, oct_h, own_h, ew_h, eb_h, cw_h, cb_h, dw_h, db_h, psi_h,
    perm_h, pmat_h, umat_h, face_h,
    vel_h,
    nb_s, oct_s, own_s, nb_v, ew, eb, cw, cb, dw, db, psi, vel, fv, cv, pool_e, pe, qe, ct, fr, fsel, fsend, enc, pooled, eup, pool_d, pd, qd, dec, sp, edge_s, far_s,
    perm, pmat, umat, faces, wt, bt, psib, psie, hots, inv, enc_p, up_p, uface,
    load_sem, out_sem, ce_s, ce_r, fe_s, fe_r, aa_s, aa_r, fx_s, fx_r, cd_s, cd_r, fd_s, fd_r, st_s, st_r,
):
    s, h = lax.axis_index("space"), lax.axis_index("chan")
    count = lax.axis_size("space")
    pos = s % WINDOW
    base = s - pos
    other = (s, 1 - h)
    after, before = s + 1, s - 1
    has_before, has_after = s > 0, s < count - 1
    has_near = jnp.where(h == 0, s, count - 1 - s) > 0
    ch = pl.ds(pl.multiple_of(16 * h, 16), 16)

    def send(src, dst, ssem, rsem, device):
        return pltpu.make_async_remote_copy(
            src_ref=src, dst_ref=dst, send_sem=ssem, recv_sem=rsem,
            device_id=device, device_id_type=pl.DeviceIdType.MESH,
        )

    barrier = pltpu.get_barrier_semaphore()
    peers = [(base + (pos + o) % WINDOW, h) for o in range(1, WINDOW)]
    def greet(device):
        pl.semaphore_signal(barrier, inc=1, device_id=device, device_id_type=pl.DeviceIdType.MESH)

    for device in [peers[o - 1] for o in (4, 12, 3, 5, 11, 13, 2, 6, 10, 14, 1, 7, 9, 15, 8)] + [other]:
        greet(device)

    @pl.when(has_before)
    def _():
        greet((before, 0))
        greet((before, 1))

    @pl.when(has_after)
    def _():
        greet((after, 0))
        greet((after, 1))

    load_f = pltpu.make_async_copy(feat, fv, load_sem.at[0])
    load_c = pltpu.make_async_copy(cfield, cv, load_sem.at[1])
    load_p = pltpu.make_async_copy(perm_h, perm, load_sem.at[15])
    load_q = pltpu.make_async_copy(face_h, faces, load_sem.at[16])
    for copy in (load_f, load_p, load_q, load_c):
        copy.start()

    def pack(rows, which, out):
        width = rows.shape[1]
        got = dot(rows.reshape(8 * width, 512), faces[which]).astype(BF).reshape(8, width, 256)
        out[0:8] = got[:, :, :128]
        for b in range(4):
            lane = iota((width, 128), 1)
            out[8 + b] = jnp.where(lane < 64, got[b, :, 128:], pltpu.roll(got[4 + b, :, 128:], 64, 1))

    def unpack(got, which, pool):
        right = [got[8 + b] for b in range(4)]
        right = right + [pltpu.roll(x, 64, 1) for x in right]
        wide = jnp.concatenate([got[0:8].reshape(256, 128), jnp.concatenate(right, axis=0)], axis=1)
        full = lax.dot_general(wide, faces[which], NT, preferred_element_type=F32)
        pool[near, :, :] = full.astype(BF).reshape(8, 32, 512)

    inner, edge = 8 * (1 - h), 8 * h
    near = pl.ds(32 + 24 * (1 - h), 8)

    ends = (
        (nb_h, nb_s), (oct_h, oct_s), (own_h, own_s), (nb_h, nb_v), (ew_h, ew), (eb_h, eb),
        (cw_h, cw), (cb_h, cb), (dw_h, dw), (db_h, db), (psi_h, psi), (pmat_h, pmat), (umat_h, umat),
    )
    small = [pltpu.make_async_copy(a, b, load_sem.at[2 + n]) for n, (a, b) in enumerate(ends)]
    for copy in small:
        copy.start()
    load_f.wait()
    load_p.wait()
    for g in range(2):
        part = fv[:, 16 * g : 16 * g + 16, :].reshape(256, 512)
        pool_e[16 * g : 16 * g + 16, ch, :] = dot(perm[...], part).astype(BF).reshape(16, 16, 512)
    load_q.wait()
    pack(pool_e[24:32, ch, :], 1, pe.at[1])
    pack(pool_e[0:8, ch, :], 0, pe.at[0])
    load_c.wait()
    for g in range(2):
        part = cv[:, 16 * g : 16 * g + 16, :].reshape(256, 512)
        ct[16 * g : 16 * g + 16] = dot(perm[...], part).astype(BF).reshape(16, 16, 512)
    extra = jnp.where(has_before, 2, 0) + jnp.where(has_after, 2, 0)
    pl.semaphore_wait(barrier, WINDOW + extra)

    face_up = send(pe.at[1], qe.at[:, ch], fe_s.at[0], fe_r.at[h], (after, 0))
    face_down = send(pe.at[0], qe.at[:, ch], fe_s.at[1], fe_r.at[h], (before, 1))
    both = send(pool_e.at[0:32, ch], pool_e.at[0:32, ch], ce_s, ce_r, other)
    spread_out = []
    for o in (1, 7, 8, 9, 15, 2, 6, 10, 14, 3, 5, 11, 13, 4, 12):
        to = (pos + o) % WINDOW
        copy = send(
            ct.at[pl.ds(2 * to, 2)], fr.at[pl.ds(2 * pos, 2)], aa_s.at[o], aa_r.at[o], (base + to, h)
        )
        copy.start()
        spread_out.append(copy)
        if o == 6:
            pl.when(has_after)(face_up.start)
            pl.when(has_before)(face_down.start)
    both.start()
    fr[pl.ds(2 * pos, 2)] = ct[pl.ds(2 * pos, 2)]

    for copy in small:
        copy.wait()
    eye = (iota((32, 32), 0) == iota((32, 32), 1)).astype(BF)
    for n, (w, b) in enumerate(((ew, eb), (cw, cb), (dw, db))):
        flat = w[...].reshape(224, 32)
        wt[n] = lax.dot_general(eye, flat, NT, preferred_element_type=F32).astype(BF)
        spread = jnp.where(iota((32, 32), 0) == iota((32, 32), 1), b[...], 0.0)
        bt[n] = jnp.broadcast_to(jnp.sum(spread, axis=1, keepdims=True), (32, 128))
    uface[...] = dot(umat[...], faces[h]).astype(BF)
    tile = (iota((32, 512), 0) == (iota((32, 512), 1) & 31)).astype(BF)
    wide = dot(psi[...], tile)
    for out, width, used in ((psib, 16, 48), (psie, 8, 24)):
        size = out.shape
        pick = [jnp.broadcast_to(wide[m : m + 1, : size[1]], (width, size[1])) for m in range(3)]
        if used < size[0]:
            pick.append(jnp.zeros((size[0] - used, size[1]), F32))
        same = (iota(size, 0) & (width - 1)) == (iota(size, 1) >> 5)
        out[...] = jnp.where(same, jnp.concatenate(pick, axis=0), 0.0).astype(BF)
    pool_e[ABSENT] = jnp.zeros((32, 512), BF)
    pool_d[ABSENT] = jnp.zeros((32, 512), BF)
    at = nb_v[...]
    rel = jnp.where(at < 0, -1, at - 32 * s + 8).astype(F32).astype(BF)
    rel = lax.dot_general(eye, rel, NT, preferred_element_type=F32)
    place = iota((32, 48), 1).astype(F32)
    for d in range(6):
        hots[d] = (place == rel[:, d : d + 1]).astype(BF)
    for kl in range(2):
        for o in range(8):
            found = jnp.int32(0)
            for child in range(8):
                hit = oct_s[16 * h + 8 * kl + child] == o
                found = jnp.where(hit, jnp.int32(8 * kl + child), found)
            inv[8 * kl + o] = found

    def fine(pool, n, out, first):
        weight, bias = wt[n], bt[n][:, :1]

        def body(t, carry):
            local = first + t
            row = 16 * h + local

            def spot(d):
                at = nb_s[d, row]
                rel = at - 32 * s
                return jnp.where(at < 0, ABSENT, rel & 63)

            spots = [spot(d) for d in range(6)]
            nb = lambda d, q: pool[spots[d], :, 128 * q : 128 * q + 128]
            out[local] = conv(quarters(pool[row]), nb, weight, bias)
            return carry

        lax.fori_loop(0, 8, body, 0, unroll=8)

    def pool_half(first):
        rows = enc[pl.ds(first, 8)].reshape(256, 512)
        pooled[pl.ds(first, 8)] = dot(rows, pmat[...]).astype(BF).reshape(8, 32, 256)

    both.wait_recv()
    fine(pool_e, 0, enc, inner)
    pool_half(inner)
    @pl.when(has_near)
    def _():
        for c in range(2):
            chc = pl.ds(16 * c, 16)
            send(pe.at[0], qe.at[:, chc], fe_s.at[0], fe_r.at[c], (s, 1 - h)).wait_recv()
        unpack(qe, 1 - h, pool_e)

    fine(pool_e, 0, enc, edge)
    pool_half(edge)
    enc_p[...] = dot(enc[pl.ds(edge, 8)].reshape(256, 512), faces[h]).astype(BF).reshape(8, 32, 256)

    for copy in spread_out:
        copy.wait_recv()
    ow = [own_s[0, n] for n in range(4)]
    slot = []
    for n in range(4):
        rank = jnp.int32(0)
        for m in range(n):
            rank = rank + jnp.where(ow[m] == ow[n], 1, 0)
        slot.append(2 * ow[n] + rank)
    for kl in range(2):
        mine = jnp.where(h == 0, slot[kl], slot[2 + kl])
        theirs = jnp.where(h == 0, slot[2 + kl], slot[kl])
        fsend[kl] = fr[theirs]
        fsel[kl, ch, :] = fr[mine]
    swap = send(fsend, fsel.at[:, ch], fx_s, fx_r, other)
    swap.start()

    def gather(kl):
        acc = [None, None]
        for o in range(8):
            part = pooled[inv[8 * kl + o]]
            step = 32 * ((o >> 1) & 1) + 4 * (o & 1)
            part = pltpu.roll(part, step, 1) if step else part
            acc[o >> 2] = part if acc[o >> 2] is None else acc[o >> 2] + part
        return jnp.concatenate(acc, axis=1)

    gathered = [gather(h), gather(1 - h)]
    swap.wait_recv()
    nothing = jnp.zeros((32, 128), BF)

    def coarse(kl, children):
        cin = (children.astype(F32) + fsel[kl].astype(F32)).astype(BF)
        cout = conv(quarters(cin), lambda d, q: nothing, wt[1], bt[1][:, :1])
        parts = []
        for o in range(8):
            part = cout[:, 256 * (o >> 2) : 256 * (o >> 2) + 256]
            step = 32 * ((o >> 1) & 1) + 4 * (o & 1)
            parts.append(pltpu.roll(part, 256 - step, 1) if step else part)
        return jnp.concatenate(parts, axis=0)

    def spread_up(kl, parts):
        up = dot(parts, umat[...])
        eup[pl.ds(8 * kl, 8)] = up.astype(BF).reshape(8, 32, 512)

    def decoder_in(first):
        def body(t, carry):
            local = first + t
            row = 16 * h + local
            up = eup[first + oct_s[row]]
            pool_d[row] = (enc[local].astype(F32) + up.astype(F32)).astype(BF)
            return carry

        lax.fori_loop(0, 8, body, 0, unroll=8)

    partner = (s + 2 * h - 1, 1 - h)
    parts = coarse(h, gathered[0])
    up_p[...] = dot(parts, uface[...]).astype(BF).reshape(8, 32, 256)
    sums = []
    for t in range(8):
        up = up_p[oct_s[16 * h + edge + t]]
        sums.append((enc_p[t].astype(F32) + up.astype(F32)).astype(BF))
        pd[t] = sums[t][:, :128]
    for b in range(4):
        lane = iota((32, 128), 1)
        pd[8 + b] = jnp.where(lane < 64, sums[b][:, 128:], pltpu.roll(sums[4 + b][:, 128:], 64, 1))
    face_d = send(pd, qd, fd_s, fd_r, partner)
    pl.when(has_near)(face_d.start)
    spread_up(h, parts)
    decoder_in(edge)
    edge_rows = pl.ds(16 * h + edge, 8)
    cross = [send(pool_d.at[edge_rows], pool_d.at[edge_rows], cd_s.at[0], cd_r.at[0], other)]
    cross[0].start()
    spread_up(1 - h, coarse(1 - h, gathered[1]))
    decoder_in(inner)
    inner_rows = pl.ds(16 * h + inner, 8)
    cross.append(send(pool_d.at[inner_rows], pool_d.at[inner_rows], cd_s.at[1], cd_r.at[1], other))
    cross[1].start()
    cross[0].wait_recv()
    cross[1].wait_recv()
    fine(pool_d, 2, dec, inner)

    @pl.when(has_near)
    def _():
        face_d.wait_recv()
        unpack(qd, 1 - h, pool_d)

    fine(pool_d, 2, dec, edge)

    edge_s[...] = dot(psie[...], dec[pl.ds(edge, 8)].reshape(256, 512)).astype(BF)
    side = s + 2 * h - 1
    far = [send(edge_s, far_s.at[1 - h], st_s.at[1 + c], st_r.at[2 - h], (side, c)) for c in range(2)]
    for copy in far:
        pl.when(has_near)(copy.start)
    own_rows = pl.ds(pl.multiple_of(16 * h, 16), 16)
    sp[:, own_rows, :] = dot(psib[...], dec[...].reshape(512, 512)).astype(BF).reshape(3, 16, 512)
    beside = send(sp.at[:, own_rows], sp.at[:, own_rows], st_s.at[0], st_r.at[0], other)
    beside.start()
    beside.wait_recv()
    for n, there in ((0, has_before), (1, has_after)):

        @pl.when(there)
        def _():
            send(edge_s, far_s.at[n], st_s.at[1], st_r.at[1 + n], other).wait_recv()

        @pl.when(jnp.logical_not(there))
        def _():
            far_s[n] = jnp.zeros((32, 512), BF)

    diff, stores = {}, []
    for m in range(3):
        axes = [a for a in range(3) if a != m]
        hot = jnp.concatenate([hots[2 * a + side_] for a in axes for side_ in range(2)], axis=0)
        mine = sp[m].astype(F32)
        lower, upper = (far_s[n].astype(F32)[8 * m : 8 * m + 8] for n in range(2))
        near_faces = dot(hot, jnp.concatenate([lower, mine, upper], axis=0).astype(BF))
        own = quarters(mine)
        pieces = {2 * a + e: quarters(near_faces[64 * n + 32 * e : 64 * n + 32 * e + 32]) for n, a in enumerate(axes) for e in range(2)}
        got = shifts(own, lambda d, q: pieces[d][q] if d in pieces else own[q])
        for a in axes:
            diff[a, m] = [0.5 * (x - y) for x, y in zip(got[2 * a + 1], got[2 * a])]
    for m in range(3):
        a, b = (m + 1) % 3, (m + 2) % 3
        vel[m] = jnp.concatenate([x - y for x, y in zip(diff[a, b], diff[b, a])], axis=1)
        stores.append(pltpu.make_async_copy(vel.at[m], vel_h.at[m], out_sem.at[m]))
        stores[m].start()

    pl.when(has_after)(face_up.wait_send)
    pl.when(has_before)(face_down.wait_send)
    for copy in spread_out + cross + [both, swap, beside]:
        copy.wait_send()
    for copy in [face_d] + far:
        pl.when(has_near)(copy.wait_send)
    for copy in stores:
        copy.wait()


def on_device(features, neighbours, octants, owners, coarse_field, ew, eb, cw, cb, dw, db, psi):
    hbm = pl.BlockSpec(memory_space=pltpu.HBM)
    dma = pltpu.SemaphoreType.DMA
    v = lambda *shape: pltpu.VMEM(shape, BF)
    f = lambda *shape: pltpu.VMEM(shape, F32)
    return pl.pallas_call(
        kernel,
        out_shape=jax.ShapeDtypeStruct((3, 32, 512), F32),
        in_specs=[hbm] * 16,
        out_specs=hbm,
        scratch_shapes=[
            pltpu.SMEM((6, 32), jnp.int32), pltpu.SMEM((32,), jnp.int32), pltpu.SMEM((1, 4), jnp.int32),
            pltpu.VMEM((6, 32), jnp.int32), v(7, 32, 32), f(1, 32), v(7, 32, 32), f(1, 32),
            v(7, 32, 32), f(1, 32), v(3, 32), f(3, 32, 512),
            v(16, 32, 512), v(16, 32, 512), v(64, 32, 512), v(2, 12, 16, 128), v(12, 32, 128),
            v(32, 16, 512), v(32, 16, 512), v(2, 32, 512), v(2, 16, 512),
            v(16, 32, 512), v(16, 32, 256), v(16, 32, 512), v(64, 32, 512), v(12, 32, 128), v(12, 32, 128),
            v(16, 32, 512), v(3, 32, 512), v(32, 512), v(2, 32, 512),
            v(256, 256), v(512, 256), v(256, 512), v(2, 512, 256), v(3, 32, 224), pltpu.VMEM((3, 32, 128), F32),
            v(48, 512), v(32, 256), v(6, 32, 48), pltpu.SMEM((16,), jnp.int32), v(8, 32, 256), v(8, 32, 256), v(256, 256),
            dma((17,)), dma((3,)), dma, dma, dma((2,)), dma((2,)), dma((16,)), dma((16,)), dma, dma,
            dma((2,)), dma((2,)), dma, dma, dma((3,)), dma((3,)),
        ],
        compiler_params=pltpu.CompilerParams(
            collective_id=0, has_side_effects=True, vmem_limit_bytes=63 * 1024 * 1024
        ),
    )(
        features, coarse_field, neighbours.T, octants, owners.reshape(1, 4),
        ew, eb.reshape(1, 32), cw, cb.reshape(1, 32), dw, db.reshape(1, 32), psi.T, *tables(),
    )


def solution(mesh):
    split, rows = P("chan", "space", None), P("space", None)
    return jax.shard_map(
        on_device,
        mesh=mesh,
        in_specs=(split, rows, P("space"), rows, split) + (P(),) * 7,
        out_specs=P(None, "space", None),
        check_vma=False,
    )
```

```python
import jax
import jax.numpy as jnp
import numpy as np
from jax import lax
from jax.experimental import pallas as pl
from jax.experimental.pallas import tpu as pltpu
from jax.sharding import PartitionSpec as P

BF = jnp.bfloat16
F32 = jnp.float32
WINDOW = 16
ABSENT = 40
NT = (((1,), (1,)), ((), ()))


def tables():
    r = np.arange(256)
    perm = (r[:, None] % 16 * 16 + r[:, None] // 16 == r[None]).astype(np.float32)
    v = np.arange(512)
    i, j, k = v // 64, v // 8 % 8, v % 8
    cell = i // 2 * 64 + j // 2 * 8 + k // 2
    place = (cell[:, None] == r[None]).astype(np.float32)
    faces = np.zeros((2, 512, 256), np.float32)
    for n, end in enumerate((0, 7)):
        on_i, on_j, on_k = i == end, j == end, k == end
        faces[n, v[on_i], (j * 8 + k)[on_i]] = 1
        on_j &= ~on_i
        faces[n, v[on_j], 64 + (i * 8 + k)[on_j]] = 1
        on_k &= ~(i == end) & ~(j == end)
        faces[n, v[on_k], 128 + (i * 8 + j)[on_k]] = 1
    return [jnp.asarray(m, BF) for m in (perm, 0.125 * place, place.T, faces)]


def iota(shape, dim):
    return lax.broadcasted_iota(jnp.int32, shape, dim)


def dot(a, b):
    return jnp.dot(a, b, preferred_element_type=F32)


def shifts(own, nb):
    lane = iota(own[0].shape, 1)
    low, j, k = lane < 64, (lane >> 3) & 7, lane & 7
    turn = lambda x, steps: pltpu.roll(x, steps, 1)
    half = [turn(x, 64) for x in own]
    minus, plus = turn(nb(0, 3), 64), turn(nb(1, 0), 64)
    four = range(4)
    return [
        [jnp.where(low, half[q - 1] if q else minus, half[q]) for q in four],
        [jnp.where(low, half[q], half[q + 1] if q < 3 else plus) for q in four],
        [jnp.where(j == 0, turn(nb(2, q), 72), turn(own[q], 8)) for q in four],
        [jnp.where(j == 7, turn(nb(3, q), 56), turn(own[q], 120)) for q in four],
        [jnp.where(k == 0, turn(nb(4, q), 121), turn(own[q], 1)) for q in four],
        [jnp.where(k == 7, turn(nb(5, q), 7), turn(own[q], 127)) for q in four],
    ]


def quarters(x):
    return [x[:, 128 * q : 128 * q + 128] for q in range(4)]


def conv(own, nb, weight, bias):
    fields = [own] + shifts(own, nb)
    taps = jnp.concatenate([jnp.concatenate(f, axis=1) for f in fields], axis=0)
    u = dot(weight, taps) + bias
    return (0.5 * u * (1.0 + jnp.tanh(0.5 * u))).astype(BF)


def kernel(
    feat, cfield, nb_h, oct_h, own_h, ew_h, eb_h, cw_h, cb_h, dw_h, db_h, psi_h,
    perm_h, pmat_h, umat_h, face_h,
    vel_h,
    nb_s, oct_s, own_s, nb_v, ew, eb, cw, cb, dw, db, psi, vel, fv, cv, pool_e, pe, qe, ct, fr, fsel, fsend, enc, pooled, eup, pool_d, pd, qd, dec, sp, edge_s, far_s,
    perm, pmat, umat, faces, wt, bt, psib, psie, hots, inv, enc_p, up_p, uface,
    load_sem, out_sem, ce_s, ce_r, fe_s, fe_r, aa_s, aa_r, fx_s, fx_r, cd_s, cd_r, fd_s, fd_r, st_s, st_r,
):
    s, h = lax.axis_index("space"), lax.axis_index("chan")
    count = lax.axis_size("space")
    pos = s % WINDOW
    base = s - pos
    other = (s, 1 - h)
    after, before = s + 1, s - 1
    has_before, has_after = s > 0, s < count - 1
    has_near = jnp.where(h == 0, s, count - 1 - s) > 0
    ch = pl.ds(pl.multiple_of(16 * h, 16), 16)

    def send(src, dst, ssem, rsem, device):
        return pltpu.make_async_remote_copy(
            src_ref=src, dst_ref=dst, send_sem=ssem, recv_sem=rsem,
            device_id=device, device_id_type=pl.DeviceIdType.MESH,
        )

    barrier = pltpu.get_barrier_semaphore()
    peers = [(base + (pos + o) % WINDOW, h) for o in range(1, WINDOW)]
    def greet(device):
        pl.semaphore_signal(barrier, inc=1, device_id=device, device_id_type=pl.DeviceIdType.MESH)

    for device in [peers[o - 1] for o in (4, 12, 3, 5, 11, 13, 2, 6, 10, 14, 1, 7, 9, 15, 8)] + [other]:
        greet(device)

    @pl.when(has_before)
    def _():
        greet((before, 0))
        greet((before, 1))

    @pl.when(has_after)
    def _():
        greet((after, 0))
        greet((after, 1))

    load_f = pltpu.make_async_copy(feat, fv, load_sem.at[0])
    load_c = pltpu.make_async_copy(cfield, cv, load_sem.at[1])
    load_p = pltpu.make_async_copy(perm_h, perm, load_sem.at[15])
    load_q = pltpu.make_async_copy(face_h, faces, load_sem.at[16])
    for copy in (load_f, load_p, load_q, load_c):
        copy.start()

    def pack(rows, which, out):
        width = rows.shape[1]
        got = dot(rows.reshape(8 * width, 512), faces[which]).astype(BF).reshape(8, width, 256)
        out[0:8] = got[:, :, :128]
        for b in range(4):
            lane = iota((width, 128), 1)
            out[8 + b] = jnp.where(lane < 64, got[b, :, 128:], pltpu.roll(got[4 + b, :, 128:], 64, 1))

    def unpack(got, which, pool):
        right = [got[8 + b] for b in range(4)]
        right = right + [pltpu.roll(x, 64, 1) for x in right]
        wide = jnp.concatenate([got[0:8].reshape(256, 128), jnp.concatenate(right, axis=0)], axis=1)
        full = lax.dot_general(wide, faces[which], NT, preferred_element_type=F32)
        pool[near, :, :] = full.astype(BF).reshape(8, 32, 512)

    inner, edge = 8 * (1 - h), 8 * h
    near = pl.ds(32 + 24 * (1 - h), 8)

    ends = (
        (nb_h, nb_s), (oct_h, oct_s), (own_h, own_s), (nb_h, nb_v), (ew_h, ew), (eb_h, eb),
        (cw_h, cw), (cb_h, cb), (dw_h, dw), (db_h, db), (psi_h, psi), (pmat_h, pmat), (umat_h, umat),
    )
    small = [pltpu.make_async_copy(a, b, load_sem.at[2 + n]) for n, (a, b) in enumerate(ends)]
    for copy in small:
        copy.start()
    load_f.wait()
    load_p.wait()
    for g in range(2):
        part = fv[:, 16 * g : 16 * g + 16, :].reshape(256, 512)
        pool_e[16 * g : 16 * g + 16, ch, :] = dot(perm[...], part).astype(BF).reshape(16, 16, 512)
    load_q.wait()
    pack(pool_e[24:32, ch, :], 1, pe.at[1])
    pack(pool_e[0:8, ch, :], 0, pe.at[0])
    load_c.wait()
    for g in range(2):
        part = cv[:, 16 * g : 16 * g + 16, :].reshape(256, 512)
        ct[16 * g : 16 * g + 16] = dot(perm[...], part).astype(BF).reshape(16, 16, 512)
    extra = jnp.where(has_before, 2, 0) + jnp.where(has_after, 2, 0)
    pl.semaphore_wait(barrier, WINDOW + extra)

    face_up = send(pe.at[1], qe.at[:, ch], fe_s.at[0], fe_r.at[h], (after, 0))
    face_down = send(pe.at[0], qe.at[:, ch], fe_s.at[1], fe_r.at[h], (before, 1))
    both = send(pool_e.at[0:32, ch], pool_e.at[0:32, ch], ce_s, ce_r, other)
    spread_out = []
    for o in (1, 7, 9, 15, 2, 6, 10, 14, 3, 5, 11, 13, 4, 12, 8):
        to = (pos + o) % WINDOW
        copy = send(
            ct.at[pl.ds(2 * to, 2)], fr.at[pl.ds(2 * pos, 2)], aa_s.at[o], aa_r.at[o], (base + to, h)
        )
        copy.start()
        spread_out.append(copy)
        if o == 10:
            pl.when(has_after)(face_up.start)
            pl.when(has_before)(face_down.start)
    both.start()
    fr[pl.ds(2 * pos, 2)] = ct[pl.ds(2 * pos, 2)]

    for copy in small:
        copy.wait()
    eye = (iota((32, 32), 0) == iota((32, 32), 1)).astype(BF)
    for n, (w, b) in enumerate(((ew, eb), (cw, cb), (dw, db))):
        flat = w[...].reshape(224, 32)
        wt[n] = lax.dot_general(eye, flat, NT, preferred_element_type=F32).astype(BF)
        spread = jnp.where(iota((32, 32), 0) == iota((32, 32), 1), b[...], 0.0)
        bt[n] = jnp.broadcast_to(jnp.sum(spread, axis=1, keepdims=True), (32, 128))
    uface[...] = dot(umat[...], faces[h]).astype(BF)
    tile = (iota((32, 512), 0) == (iota((32, 512), 1) & 31)).astype(BF)
    wide = dot(psi[...], tile)
    for out, width, used in ((psib, 16, 48), (psie, 8, 24)):
        size = out.shape
        pick = [jnp.broadcast_to(wide[m : m + 1, : size[1]], (width, size[1])) for m in range(3)]
        if used < size[0]:
            pick.append(jnp.zeros((size[0] - used, size[1]), F32))
        same = (iota(size, 0) & (width - 1)) == (iota(size, 1) >> 5)
        out[...] = jnp.where(same, jnp.concatenate(pick, axis=0), 0.0).astype(BF)
    pool_e[ABSENT] = jnp.zeros((32, 512), BF)
    pool_d[ABSENT] = jnp.zeros((32, 512), BF)
    at = nb_v[...]
    rel = jnp.where(at < 0, -1, at - 32 * s + 8).astype(F32).astype(BF)
    rel = lax.dot_general(eye, rel, NT, preferred_element_type=F32)
    place = iota((32, 48), 1).astype(F32)
    for d in range(6):
        hots[d] = (place == rel[:, d : d + 1]).astype(BF)
    for kl in range(2):
        for o in range(8):
            found = jnp.int32(0)
            for child in range(8):
                hit = oct_s[16 * h + 8 * kl + child] == o
                found = jnp.where(hit, jnp.int32(8 * kl + child), found)
            inv[8 * kl + o] = found

    def fine(pool, n, out, first):
        weight, bias = wt[n], bt[n][:, :1]

        def body(t, carry):
            local = first + t
            row = 16 * h + local

            def spot(d):
                at = nb_s[d, row]
                rel = at - 32 * s
                return jnp.where(at < 0, ABSENT, rel & 63)

            spots = [spot(d) for d in range(6)]
            nb = lambda d, q: pool[spots[d], :, 128 * q : 128 * q + 128]
            out[local] = conv(quarters(pool[row]), nb, weight, bias)
            return carry

        lax.fori_loop(0, 8, body, 0, unroll=8)

    def pool_half(first):
        rows = enc[pl.ds(first, 8)].reshape(256, 512)
        pooled[pl.ds(first, 8)] = dot(rows, pmat[...]).astype(BF).reshape(8, 32, 256)

    both.wait_recv()
    fine(pool_e, 0, enc, inner)
    pool_half(inner)
    @pl.when(has_near)
    def _():
        for c in range(2):
            chc = pl.ds(16 * c, 16)
            send(pe.at[0], qe.at[:, chc], fe_s.at[0], fe_r.at[c], (s, 1 - h)).wait_recv()
        unpack(qe, 1 - h, pool_e)

    fine(pool_e, 0, enc, edge)
    pool_half(edge)
    enc_p[...] = dot(enc[pl.ds(edge, 8)].reshape(256, 512), faces[h]).astype(BF).reshape(8, 32, 256)

    for copy in spread_out:
        copy.wait_recv()
    ow = [own_s[0, n] for n in range(4)]
    slot = []
    for n in range(4):
        rank = jnp.int32(0)
        for m in range(n):
            rank = rank + jnp.where(ow[m] == ow[n], 1, 0)
        slot.append(2 * ow[n] + rank)
    for kl in range(2):
        mine = jnp.where(h == 0, slot[kl], slot[2 + kl])
        theirs = jnp.where(h == 0, slot[2 + kl], slot[kl])
        fsend[kl] = fr[theirs]
        fsel[kl, ch, :] = fr[mine]
    swap = send(fsend, fsel.at[:, ch], fx_s, fx_r, other)
    swap.start()

    def gather(kl):
        acc = [None, None]
        for o in range(8):
            part = pooled[inv[8 * kl + o]]
            step = 32 * ((o >> 1) & 1) + 4 * (o & 1)
            part = pltpu.roll(part, step, 1) if step else part
            acc[o >> 2] = part if acc[o >> 2] is None else acc[o >> 2] + part
        return jnp.concatenate(acc, axis=1)

    gathered = [gather(h), gather(1 - h)]
    swap.wait_recv()
    nothing = jnp.zeros((32, 128), BF)

    def coarse(kl, children):
        cin = (children.astype(F32) + fsel[kl].astype(F32)).astype(BF)
        cout = conv(quarters(cin), lambda d, q: nothing, wt[1], bt[1][:, :1])
        parts = []
        for o in range(8):
            part = cout[:, 256 * (o >> 2) : 256 * (o >> 2) + 256]
            step = 32 * ((o >> 1) & 1) + 4 * (o & 1)
            parts.append(pltpu.roll(part, 256 - step, 1) if step else part)
        return jnp.concatenate(parts, axis=0)

    def spread_up(kl, parts):
        up = dot(parts, umat[...])
        eup[pl.ds(8 * kl, 8)] = up.astype(BF).reshape(8, 32, 512)

    def decoder_in(first):
        def body(t, carry):
            local = first + t
            row = 16 * h + local
            up = eup[first + oct_s[row]]
            pool_d[row] = (enc[local].astype(F32) + up.astype(F32)).astype(BF)
            return carry

        lax.fori_loop(0, 8, body, 0, unroll=8)

    partner = (s + 2 * h - 1, 1 - h)
    parts = coarse(h, gathered[0])
    up_p[...] = dot(parts, uface[...]).astype(BF).reshape(8, 32, 256)
    sums = []
    for t in range(8):
        up = up_p[oct_s[16 * h + edge + t]]
        sums.append((enc_p[t].astype(F32) + up.astype(F32)).astype(BF))
        pd[t] = sums[t][:, :128]
    for b in range(4):
        lane = iota((32, 128), 1)
        pd[8 + b] = jnp.where(lane < 64, sums[b][:, 128:], pltpu.roll(sums[4 + b][:, 128:], 64, 1))
    face_d = send(pd, qd, fd_s, fd_r, partner)
    pl.when(has_near)(face_d.start)
    spread_up(h, parts)
    decoder_in(edge)
    edge_rows = pl.ds(16 * h + edge, 8)
    cross = [send(pool_d.at[edge_rows], pool_d.at[edge_rows], cd_s.at[0], cd_r.at[0], other)]
    cross[0].start()
    spread_up(1 - h, coarse(1 - h, gathered[1]))
    decoder_in(inner)
    inner_rows = pl.ds(16 * h + inner, 8)
    cross.append(send(pool_d.at[inner_rows], pool_d.at[inner_rows], cd_s.at[1], cd_r.at[1], other))
    cross[1].start()
    cross[0].wait_recv()
    cross[1].wait_recv()
    fine(pool_d, 2, dec, inner)

    @pl.when(has_near)
    def _():
        face_d.wait_recv()
        unpack(qd, 1 - h, pool_d)

    fine(pool_d, 2, dec, edge)

    edge_s[...] = dot(psie[...], dec[pl.ds(edge, 8)].reshape(256, 512)).astype(BF)
    side = s + 2 * h - 1
    far = [send(edge_s, far_s.at[1 - h], st_s.at[1 + c], st_r.at[2 - h], (side, c)) for c in range(2)]
    for copy in far:
        pl.when(has_near)(copy.start)
    own_rows = pl.ds(pl.multiple_of(16 * h, 16), 16)
    sp[:, own_rows, :] = dot(psib[...], dec[...].reshape(512, 512)).astype(BF).reshape(3, 16, 512)
    beside = send(sp.at[:, own_rows], sp.at[:, own_rows], st_s.at[0], st_r.at[0], other)
    beside.start()
    beside.wait_recv()
    for n, there in ((0, has_before), (1, has_after)):

        @pl.when(there)
        def _():
            send(edge_s, far_s.at[n], st_s.at[1], st_r.at[1 + n], other).wait_recv()

        @pl.when(jnp.logical_not(there))
        def _():
            far_s[n] = jnp.zeros((32, 512), BF)

    diff, stores = {}, []
    for m in range(3):
        axes = [a for a in range(3) if a != m]
        hot = jnp.concatenate([hots[2 * a + side_] for a in axes for side_ in range(2)], axis=0)
        mine = sp[m].astype(F32)
        lower, upper = (far_s[n].astype(F32)[8 * m : 8 * m + 8] for n in range(2))
        near_faces = dot(hot, jnp.concatenate([lower, mine, upper], axis=0).astype(BF))
        own = quarters(mine)
        pieces = {2 * a + e: quarters(near_faces[64 * n + 32 * e : 64 * n + 32 * e + 32]) for n, a in enumerate(axes) for e in range(2)}
        got = shifts(own, lambda d, q: pieces[d][q] if d in pieces else own[q])
        for a in axes:
            diff[a, m] = [0.5 * (x - y) for x, y in zip(got[2 * a + 1], got[2 * a])]
    for m in range(3):
        a, b = (m + 1) % 3, (m + 2) % 3
        vel[m] = jnp.concatenate([x - y for x, y in zip(diff[a, b], diff[b, a])], axis=1)
        stores.append(pltpu.make_async_copy(vel.at[m], vel_h.at[m], out_sem.at[m]))
        stores[m].start()

    pl.when(has_after)(face_up.wait_send)
    pl.when(has_before)(face_down.wait_send)
    for copy in spread_out + cross + [both, swap, beside]:
        copy.wait_send()
    for copy in [face_d] + far:
        pl.when(has_near)(copy.wait_send)
    for copy in stores:
        copy.wait()


def on_device(features, neighbours, octants, owners, coarse_field, ew, eb, cw, cb, dw, db, psi):
    hbm = pl.BlockSpec(memory_space=pltpu.HBM)
    dma = pltpu.SemaphoreType.DMA
    v = lambda *shape: pltpu.VMEM(shape, BF)
    f = lambda *shape: pltpu.VMEM(shape, F32)
    return pl.pallas_call(
        kernel,
        out_shape=jax.ShapeDtypeStruct((3, 32, 512), F32),
        in_specs=[hbm] * 16,
        out_specs=hbm,
        scratch_shapes=[
            pltpu.SMEM((6, 32), jnp.int32), pltpu.SMEM((32,), jnp.int32), pltpu.SMEM((1, 4), jnp.int32),
            pltpu.VMEM((6, 32), jnp.int32), v(7, 32, 32), f(1, 32), v(7, 32, 32), f(1, 32),
            v(7, 32, 32), f(1, 32), v(3, 32), f(3, 32, 512),
            v(16, 32, 512), v(16, 32, 512), v(64, 32, 512), v(2, 12, 16, 128), v(12, 32, 128),
            v(32, 16, 512), v(32, 16, 512), v(2, 32, 512), v(2, 16, 512),
            v(16, 32, 512), v(16, 32, 256), v(16, 32, 512), v(64, 32, 512), v(12, 32, 128), v(12, 32, 128),
            v(16, 32, 512), v(3, 32, 512), v(32, 512), v(2, 32, 512),
            v(256, 256), v(512, 256), v(256, 512), v(2, 512, 256), v(3, 32, 224), pltpu.VMEM((3, 32, 128), F32),
            v(48, 512), v(32, 256), v(6, 32, 48), pltpu.SMEM((16,), jnp.int32), v(8, 32, 256), v(8, 32, 256), v(256, 256),
            dma((17,)), dma((3,)), dma, dma, dma((2,)), dma((2,)), dma((16,)), dma((16,)), dma, dma,
            dma((2,)), dma((2,)), dma, dma, dma((3,)), dma((3,)),
        ],
        compiler_params=pltpu.CompilerParams(
            collective_id=0, has_side_effects=True, vmem_limit_bytes=63 * 1024 * 1024
        ),
    )(
        features, coarse_field, neighbours.T, octants, owners.reshape(1, 4),
        ew, eb.reshape(1, 32), cw, cb.reshape(1, 32), dw, db.reshape(1, 32), psi.T, *tables(),
    )


def solution(mesh):
    split, rows = P("chan", "space", None), P("space", None)
    return jax.shard_map(
        on_device,
        mesh=mesh,
        in_specs=(split, rows, P("space"), rows, split) + (P(),) * 7,
        out_specs=P(None, "space", None),
        check_vma=False,
    )
```
